32 devices in a mesh: pb: 4 (over y, core), ka: 2 (over x), ha: 4 (over z).
Axes of the slice: x: 2, y: 2, z: 4, core: 2. Of those that a mesh axis runs over, the one named last changes fastest.
Arguments:
- queries: bfloat16 [2048, 512], P(('pb', 'ka'), 'ha'), may hold values from -6 to 6
- key_rows: bfloat16 [2048, 512], P(('pb', 'ka'), 'ha'), may hold values from -6 to 6
- value_rows: bfloat16 [2048, 512], P(('pb', 'ka'), 'ha'), may hold values from -6 to 6
- outputs: bfloat16 [2048, 512], P(('pb', 'ka'), 'ha'), may hold values from -6 to 6
- out_grad: bfloat16 [2048, 512], P(('pb', 'ka'), 'ha'), may hold values from -6 to 6
- saved_lse: bfloat16 [2048, 4], P(('pb', 'ka'), 'ha'), may hold values from -1 to 12, as said below
- fold_map: int32 [16], replicated, may hold values from 0 to 15, as said below
Outputs:
- query_grad: bfloat16 [2048, 512], P(('pb', 'ka'), 'ha')
- key_grad: bfloat16 [2048, 512], P(('pb', 'ka'), 'ha')
- value_grad: bfloat16 [2048, 512], P(('pb', 'ka'), 'ha')
The draws below stay inside these ranges and needn't reach their ends.
Inputs may be any that keep to these rules, and one draw needn't show every extreme that they name: `fold_map`: stored blocks 2 d and 2 d + 1 hold a mirrored pair of blocks, b and 15 - b, in either order; every block is held once. `saved_lse`: close to the log-sum-exp of the row's visible scores.
All inputs are finite; a program needn't handle non-finite values.
Results may differ from the reference program's by a relative error of at most 0.0055.
Values may be sent and summed in bfloat16 or wider, within the bound.
A program may use at most 64 MiB of HBM per device.

```python
import math
import jax
import jax.numpy as jnp
from jax import lax

HEAD_DIM = 128
HEADS = 4
SEQ = 2048
BLOCK_ROWS = 128
BLOCKS = 16
WIDTH = 512


def fold_blocks(key):
    pair_count = BLOCKS // 2
    pair_order = jax.random.permutation(jax.random.fold_in(key, 11), pair_count).astype(jnp.int32)
    flipped = jax.random.randint(jax.random.fold_in(key, 13), (pair_count,), 0, 2).astype(jnp.int32)
    first_block = jnp.where(flipped == 1, BLOCKS - 1 - pair_order, pair_order)
    second_block = BLOCKS - 1 - first_block
    return jnp.stack([first_block, second_block], axis=1).reshape(BLOCKS).astype(jnp.int32)


def draw_fold_map(key, part):
    return fold_blocks(key)


def draw_saved_lse(key, part):
    ordering = fold_blocks(key)
    key = jax.random.fold_in(key, 7)
    slots = jnp.arange(SEQ, dtype=jnp.int32)
    position = ordering[slots // BLOCK_ROWS] * BLOCK_ROWS + slots % BLOCK_ROWS
    center = jnp.log(position.astype(jnp.float32) + 1.0) + 0.5
    noise = 0.3 * jax.random.truncated_normal(key, -2.0, 2.0, (SEQ, HEADS), jnp.float32)
    return (center[:, None] + noise).astype(jnp.bfloat16)


def block_levels(rng, dims, shards, low, top_value):
    loudness = 1.0
    for axis_at, blocks in shards:
        heights = jax.random.uniform(jax.random.fold_in(jax.random.fold_in(rng, 6), axis_at), (blocks,), jnp.float32, low / len(shards), top_value / len(shards))
        loudness = loudness * jnp.repeat(jnp.exp(heights), dims[axis_at] // blocks).reshape((-1,) + (1,) * (len(dims) - 1 - axis_at))
    return loudness


def gaussian(rng, extent, deviation, most, split=(), kind=jnp.bfloat16):
    loudness = block_levels(rng, extent, split, -0.22, 0.18) if split else 1.0
    values = jax.random.normal(rng, extent, jnp.float32) * deviation * loudness
    return jnp.minimum(jnp.maximum(values, -most), most).astype(kind)


def setup_inputs(seed: int = 0) -> dict:
    splits = jax.random.split(jax.random.key(seed), 8)
    queries = gaussian(splits[0], (SEQ, WIDTH), 1.0, 6.0, ((0, 8), (1, 4)))
    key_rows = gaussian(splits[1], (SEQ, WIDTH), 1.0, 6.0, ((0, 8), (1, 4)))
    value_rows = gaussian(splits[2], (SEQ, WIDTH), 1.0, 6.0, ((0, 8), (1, 4)))
    outputs = gaussian(splits[3], (SEQ, WIDTH), 1.0, 6.0, ((0, 8), (1, 4)))
    out_grad = gaussian(splits[4], (SEQ, WIDTH), 1.0, 6.0, ((0, 8), (1, 4)))
    saved_lse = draw_saved_lse(jax.random.fold_in(splits[7], 71), 0)
    fold_map = draw_fold_map(jax.random.fold_in(splits[7], 71), 0)
    return dict(queries=queries, key_rows=key_rows, value_rows=value_rows, outputs=outputs, out_grad=out_grad, saved_lse=saved_lse, fold_map=fold_map)


def reference(queries, key_rows, value_rows, outputs, out_grad, saved_lse, fold_map):
    factor = 1.0 / math.sqrt(HEAD_DIM)
    seq_len = queries.shape[0]
    slots = jnp.arange(seq_len, dtype=jnp.int32)
    position = fold_map[slots // BLOCK_ROWS] * BLOCK_ROWS + slots % BLOCK_ROWS
    shaped = (seq_len, HEADS, HEAD_DIM)
    query_all = queries.reshape(shaped).astype(jnp.float32)
    key_all = key_rows.reshape(shaped).astype(jnp.float32)
    value_all = value_rows.reshape(shaped).astype(jnp.float32)
    grad_all = out_grad.reshape(shaped).astype(jnp.float32)
    saved_all = outputs.reshape(shaped).astype(jnp.float32)
    delta = jnp.einsum('qhd,qhd->qh', grad_all, saved_all).astype(jnp.bfloat16)
    delta = lax.optimization_barrier(delta).astype(jnp.float32)
    lse_all = saved_lse.astype(jnp.float32)
    block_len = math.gcd(seq_len, 512)

    def one_block(totals, number):
        key_sum, value_sum = totals
        first_row = (number * block_len).astype(jnp.int32)
        query_blk = lax.dynamic_slice_in_dim(query_all, first_row, block_len, 0)
        grad_blk = lax.dynamic_slice_in_dim(grad_all, first_row, block_len, 0)
        lse_blk = lax.dynamic_slice_in_dim(lse_all, first_row, block_len, 0)
        delta_blk = lax.dynamic_slice_in_dim(delta, first_row, block_len, 0)
        query_pos = lax.dynamic_slice_in_dim(position, first_row, block_len, 0)
        scores = jnp.einsum('qhd,khd->hqk', query_blk, key_all) * factor
        visible = position[None, :] <= query_pos[:, None]
        probs = jnp.where(visible[None], jnp.exp(scores - lse_blk.T[:, :, None]), 0.0)
        probs_low = lax.optimization_barrier(probs.astype(jnp.bfloat16)).astype(jnp.float32)
        value_sum = value_sum + jnp.einsum('hqk,qhd->khd', probs_low, grad_blk)
        dprobs = jnp.einsum('qhd,khd->hqk', grad_blk, value_all)
        dscores = probs * (dprobs - delta_blk.T[:, :, None])
        dscores_low = lax.optimization_barrier(dscores.astype(jnp.bfloat16)).astype(jnp.float32)
        query_part = jnp.einsum('hqk,khd->qhd', dscores_low, key_all)
        key_sum = key_sum + jnp.einsum('hqk,qhd->khd', dscores_low, query_blk)
        return ((key_sum, value_sum), query_part)
    empty = jnp.zeros(shaped, jnp.float32)
    totals, parts = lax.scan(one_block, (empty, empty), jnp.arange(seq_len // block_len, dtype=jnp.int32))
    full_width = HEADS * HEAD_DIM
    query_grad = (parts.reshape(seq_len, full_width) * factor).astype(jnp.bfloat16)
    key_grad = (totals[0].reshape(seq_len, full_width) * factor).astype(jnp.bfloat16)
    value_grad = totals[1].reshape(seq_len, full_width).astype(jnp.bfloat16)
    return (query_grad, key_grad, value_grad)
```

```python
import functools
import math

import jax
import jax.numpy as jnp
from jax import lax
from jax.experimental import pallas as pl
from jax.experimental.pallas import tpu as pltpu
from jax.sharding import PartitionSpec as P


def block_length(row_total):
    length = row_total
    while length > 512 and length % 2 == 0:
        length = length // 2
    return length


def tile_grads(
    query_blk, grad_blk, lse_blk, delta_blk, query_pos, key_blk, value_blk, key_pos, factor
):
    scores = (
        jnp.einsum("qhd,khd->hqk", query_blk, key_blk, preferred_element_type=jnp.float32) * factor
    )
    visible = key_pos[None, :] <= query_pos[:, None]
    probs = jnp.where(visible[None], jnp.exp(scores - lse_blk.T[:, :, None]), 0.0)
    probs_low = probs.astype(jnp.bfloat16)
    value_part = jnp.einsum("hqk,qhd->khd", probs_low, grad_blk, preferred_element_type=jnp.float32)
    dprobs = jnp.einsum("qhd,khd->hqk", grad_blk, value_blk, preferred_element_type=jnp.float32)
    dscores = (probs * (dprobs - delta_blk.T[:, :, None])).astype(jnp.bfloat16)
    query_part = jnp.einsum("hqk,khd->qhd", dscores, key_blk, preferred_element_type=jnp.float32)
    key_part = jnp.einsum("hqk,qhd->khd", dscores, query_blk, preferred_element_type=jnp.float32)
    return (query_part, key_part, value_part)


def add_rows(target, update, first_row):
    length = update.shape[0]
    current = lax.dynamic_slice_in_dim(target, first_row, length, 0)
    return lax.dynamic_update_slice_in_dim(target, current + update, first_row, 0)


def body(queries, key_rows, value_rows, outputs, out_grad, saved_lse, fold_map):
    row_count, full_width = queries.shape
    head_count = saved_lse.shape[1]
    head_dim = full_width // head_count
    factor = 1.0 / math.sqrt(head_dim)
    fold_rows = row_count // 2
    size_pb = lax.axis_size("pb")
    size_ka = lax.axis_size("ka")
    index_pb = lax.axis_index("pb")
    index_ka = lax.axis_index("ka")
    key_all, value_all = (
        lax.all_gather(key_rows, "pb", axis=0, tiled=True),
        lax.all_gather(value_rows, "pb", axis=0, tiled=True),
    )
    key_len = size_pb * row_count
    key_all = key_all.reshape(key_len, head_count, head_dim)
    value_all = value_all.reshape(key_len, head_count, head_dim)
    key_iota = jnp.arange(key_len, dtype=jnp.int32)
    key_global = (key_iota // row_count * size_ka + index_ka) * row_count + key_iota % row_count
    key_pos = fold_map[key_global // fold_rows] * fold_rows + key_global % fold_rows
    query_len = size_ka * row_count
    query_first = index_pb * query_len
    query_empty = jnp.zeros((query_len, head_count, head_dim), jnp.float32)
    key_empty = jnp.zeros((key_len, head_count, head_dim), jnp.float32)
    init = (query_empty, key_empty, key_empty)
    query_src = lax.all_gather(queries, "ka", axis=0, tiled=True)
    grad_src = lax.all_gather(out_grad, "ka", axis=0, tiled=True)
    saved_src = lax.all_gather(outputs, "ka", axis=0, tiled=True)
    lse_src = lax.all_gather(saved_lse, "ka", axis=0, tiled=True)
    piece_rows = query_src.shape[0]
    step_rows = block_length(piece_rows)

    def one_block(number, state):
        dq_all, dk_all, dv_all = state
        offset = number * step_rows
        query_blk = lax.dynamic_slice_in_dim(query_src, offset, step_rows, 0).reshape(
            step_rows, head_count, head_dim
        )
        grad_blk = lax.dynamic_slice_in_dim(grad_src, offset, step_rows, 0).reshape(
            step_rows, head_count, head_dim
        )
        lse_blk = lax.dynamic_slice_in_dim(lse_src, offset, step_rows, 0).astype(jnp.float32)
        saved_blk = lax.dynamic_slice_in_dim(saved_src, offset, step_rows, 0).reshape(
            step_rows, head_count, head_dim
        )
        delta_low = jnp.einsum(
            "qhd,qhd->qh", grad_blk, saved_blk, preferred_element_type=jnp.float32
        ).astype(jnp.bfloat16)
        delta_blk = lax.optimization_barrier(delta_low).astype(jnp.float32)
        row_global = query_first + offset + jnp.arange(step_rows, dtype=jnp.int32)
        query_pos = fold_map[row_global // fold_rows] * fold_rows + row_global % fold_rows
        dq_blk, dk_part, dv_part = tile_grads(
            query_blk, grad_blk, lse_blk, delta_blk, query_pos, key_all, value_all, key_pos, factor
        )
        dk_all = dk_all + dk_part
        dv_all = dv_all + dv_part
        dq_all = add_rows(dq_all, dq_blk, offset)
        return (dq_all, dk_all, dv_all)

    dq_all, dk_all, dv_all = lax.fori_loop(0, piece_rows // step_rows, one_block, init)
    query_mine = lax.psum_scatter(
        dq_all.reshape(query_len, full_width), "ka", scatter_dimension=0, tiled=True
    )
    query_grad = (query_mine * factor).astype(jnp.bfloat16)
    key_flat = dk_all.reshape(key_len, full_width)
    value_flat = dv_all.reshape(key_len, full_width)
    key_total, value_total = lax.psum((key_flat, value_flat), "pb")
    key_mine = lax.dynamic_slice_in_dim(key_total, index_pb * row_count, row_count, 0)
    value_mine = lax.dynamic_slice_in_dim(value_total, index_pb * row_count, row_count, 0)
    key_grad = (key_mine * factor).astype(jnp.bfloat16)
    value_grad = value_mine.astype(jnp.bfloat16)
    return (query_grad, key_grad, value_grad)


MESH = pl.DeviceIdType.MESH
NT = (((1,), (1,)), ((), ()))
TN = (((0,), (0,)), ((), ()))


def plane_kernel(
    rows, factor,
    q_in, k_in, v_in, o_in, g_in, lse_in, map_in,
    dq_out, dk_out, dv_out,
    q_buf, g_buf, k_buf, v_buf, o_buf, lse_buf, map_buf, stat,
    dq_acc, dk_acc, dv_acc,
    kv_send, kv_recv, qc_send, qc_recv, qx_send, qx_recv,
    local_sem, send_sem, recv_sem,
):
    p = lax.axis_index("pb")
    x = lax.axis_index("ka")
    h = lax.axis_index("ha")
    c = lax.rem(p, 2)
    y = p // 2
    p_core = p + 1 - 2 * c
    p_far = lax.rem(p + 2, 4)
    to_core = (p_core, x, h)
    to_x = (p, 1 - x, h)
    to_y = (p_far, x, h)
    to_both = (p_core, 1 - x, h)
    fold_rows = rows // 2

    def part(slot):
        return pl.ds(slot * rows, rows)

    locals_ = []
    for n, (src, dst) in enumerate((
        (g_in, g_buf.at[part(0)]), (o_in, o_buf), (lse_in, lse_buf), (q_in, q_buf.at[part(0)]),
        (k_in, k_buf.at[part(0)]), (v_in, v_buf.at[part(0)]), (map_in, map_buf),
    )):
        copy = pltpu.make_async_copy(src, dst, local_sem.at[n])
        copy.start()
        locals_.append(copy)

    barrier = pltpu.get_barrier_semaphore()
    for peer in (to_core, to_x, to_y, to_both):
        pl.semaphore_signal(barrier, inc=1, device_id=peer, device_id_type=MESH)
    pl.semaphore_wait(barrier, 4)

    sends = []

    def send(n, src, dst, peer):
        copy = pltpu.make_async_remote_copy(
            src_ref=src, dst_ref=dst, send_sem=send_sem.at[n], recv_sem=recv_sem.at[n],
            device_id=peer, device_id_type=MESH,
        )
        copy.start()
        sends.append(copy)
        return copy

    q_x = send(0, q_in, q_buf.at[part(2)], to_x)
    k_y = send(1, k_in, k_buf.at[part(1)], to_y)
    q_c = send(2, q_in, q_buf.at[part(1)], to_core)
    g_c = send(3, g_in, g_buf.at[part(1)], to_core)
    g_x = send(4, g_in, g_buf.at[part(2)], to_x)
    v_y = send(5, v_in, v_buf.at[part(1)], to_y)

    for copy in locals_[:3]:
        copy.wait()
    gram = lax.dot_general(o_buf[...], g_buf[part(0)], NT, preferred_element_type=jnp.float32)
    down = lax.broadcasted_iota(jnp.int32, (rows, rows), 0)
    along = lax.broadcasted_iota(jnp.int32, (rows, rows), 1)
    delta = jnp.sum(jnp.where(down == along, gram, 0.0), axis=0, keepdims=True)
    delta = delta.astype(jnp.bfloat16).astype(jnp.float32)
    log2e = math.log2(math.e)
    lse = lse_buf[...].astype(jnp.float32) * log2e
    which = lax.broadcasted_iota(jnp.int32, (8, rows), 0)
    stat[0] = jnp.where(which == 0, lse, delta)
    st_c = send(6, stat.at[0], stat.at[1], to_core)
    st_x = send(7, stat.at[0], stat.at[2], to_x)
    st_b = send(8, stat.at[0], stat.at[3], to_both)
    for copy in locals_[3:]:
        copy.wait()

    lane = lax.broadcasted_iota(jnp.int32, (1, fold_rows), 1)
    level = lax.broadcasted_iota(jnp.int32, (fold_rows, 1), 0)
    q_owner = (p * 2 + x, p_core * 2 + x, p * 2 + 1 - x, p_core * 2 + 1 - x)
    k_owner = (p * 2 + x, p_far * 2 + x)

    def tile(j, s, first_q, first_k):
        keys, values = k_buf[part(j)], v_buf[part(j)]
        query, grad = q_buf[part(s)], g_buf[part(s)]
        k_pos = jnp.concatenate(
            [map_buf[k_owner[j] * 2 + i] * fold_rows + level for i in range(2)], axis=0)
        q_pos = jnp.concatenate(
            [map_buf[q_owner[s] * 2 + i] * fold_rows + lane for i in range(2)], axis=1)
        scores = lax.dot_general(keys, query, NT, preferred_element_type=jnp.float32)
        probs = jnp.where(
            k_pos <= q_pos, jnp.exp2(scores * (factor * log2e) - stat[s, 0:1, :]), 0.0)
        dv = jnp.dot(probs.astype(jnp.bfloat16), grad, preferred_element_type=jnp.float32)
        dprobs = lax.dot_general(values, grad, NT, preferred_element_type=jnp.float32)
        dscores = (probs * (dprobs - stat[s, 1:2, :])).astype(jnp.bfloat16)
        dk = jnp.dot(dscores, query, preferred_element_type=jnp.float32)
        dq = lax.dot_general(dscores, keys, TN, preferred_element_type=jnp.float32)
        dv_acc[part(j)] = dv if first_k else dv_acc[part(j)] + dv
        dk_acc[part(j)] = dk if first_k else dk_acc[part(j)] + dk
        dq_acc[part(s)] = dq if first_q else dq_acc[part(s)] + dq

    tile(0, 0, True, True)
    q_c.wait_recv()
    g_c.wait_recv()
    st_c.wait_recv()
    tile(0, 1, True, False)
    q_x.wait_recv()
    q_r = send(9, q_buf.at[part(2)], q_buf.at[part(3)], to_core)
    k_y.wait_recv()
    g_x.wait_recv()
    g_r = send(10, g_buf.at[part(2)], g_buf.at[part(3)], to_core)
    v_y.wait_recv()
    tile(1, 0, False, True)
    tile(1, 1, False, False)
    qc_send[0] = dq_acc[part(1)].astype(jnp.bfloat16)
    dq_c0 = send(11, qc_send.at[0], qc_recv.at[0], to_core)
    st_x.wait_recv()
    tile(1, 2, True, False)
    q_r.wait_recv()
    g_r.wait_recv()
    st_b.wait_recv()
    tile(1, 3, True, False)
    kv_send[0] = dv_acc[part(1)].astype(jnp.bfloat16)
    dv_y = send(12, kv_send.at[0], kv_recv.at[0], to_y)
    kv_send[1] = dk_acc[part(1)].astype(jnp.bfloat16)
    dk_y = send(13, kv_send.at[1], kv_recv.at[1], to_y)
    tile(0, 3, False, False)
    qc_send[1] = dq_acc[part(3)].astype(jnp.bfloat16)
    dq_c1 = send(14, qc_send.at[1], qc_recv.at[1], to_core)
    tile(0, 2, False, False)
    dq_c1.wait_recv()
    qx_send[...] = (dq_acc[part(2)] + qc_recv[1].astype(jnp.float32)).astype(jnp.bfloat16)
    dq_x = send(15, qx_send, qx_recv, to_x)
    dq_c0.wait_recv()
    dq_mine = dq_acc[part(0)] + qc_recv[0].astype(jnp.float32)
    dv_y.wait_recv()
    dv_out[...] = (dv_acc[part(0)] + kv_recv[0].astype(jnp.float32)).astype(jnp.bfloat16)
    dk_y.wait_recv()
    dk_out[...] = (
        (dk_acc[part(0)] + kv_recv[1].astype(jnp.float32)) * factor).astype(jnp.bfloat16)
    dq_x.wait_recv()
    dq_out[...] = ((dq_mine + qx_recv[...].astype(jnp.float32)) * factor).astype(jnp.bfloat16)
    for copy in sends:
        copy.wait_send()


def plane_body(queries, key_rows, value_rows, outputs, out_grad, saved_lse, fold_map):
    rows, width = queries.shape
    factor = 1.0 / math.sqrt(width)
    low, full = jnp.bfloat16, jnp.float32
    grad = jax.ShapeDtypeStruct((rows, width), low)
    return pl.pallas_call(
        functools.partial(plane_kernel, rows, factor),
        out_shape=(grad, grad, grad),
        in_specs=[pl.BlockSpec(memory_space=pl.ANY)] * 7,
        out_specs=[pl.BlockSpec(memory_space=pltpu.VMEM)] * 3,
        scratch_shapes=[
            pltpu.VMEM((4 * rows, width), low),
            pltpu.VMEM((4 * rows, width), low),
            pltpu.VMEM((2 * rows, width), low),
            pltpu.VMEM((2 * rows, width), low),
            pltpu.VMEM((rows, width), low),
            pltpu.VMEM((1, rows), low),
            pltpu.SMEM(fold_map.shape, jnp.int32),
            pltpu.VMEM((4, 8, rows), full),
            pltpu.VMEM((4 * rows, width), full),
            pltpu.VMEM((2 * rows, width), full),
            pltpu.VMEM((2 * rows, width), full),
            pltpu.VMEM((2, rows, width), low),
            pltpu.VMEM((2, rows, width), low),
            pltpu.VMEM((2, rows, width), low),
            pltpu.VMEM((2, rows, width), low),
            pltpu.VMEM((rows, width), low),
            pltpu.VMEM((rows, width), low),
            pltpu.SemaphoreType.DMA((7,)),
            pltpu.SemaphoreType.DMA((16,)),
            pltpu.SemaphoreType.DMA((16,)),
        ],
        compiler_params=pltpu.CompilerParams(
            collective_id=0, has_side_effects=True, vmem_limit_bytes=32 * 2**20
        ),
        cost_estimate=pl.CostEstimate(
            flops=80 * rows * rows * width,
            bytes_accessed=16 * rows * width,
            transcendentals=8 * rows * rows,
        ),
    )(queries, key_rows, value_rows, outputs, out_grad, saved_lse.reshape(1, rows), fold_map)


def solution(mesh):
    plane = mesh.shape["pb"] == 4 and mesh.shape["ka"] == 2
    return jax.shard_map(
        plane_body if plane else body,
        mesh=mesh,
        in_specs=(
            P(("pb", "ka"), "ha"),
            P(("pb", "ka"), "ha"),
            P(("pb", "ka"), "ha"),
            P(("pb", "ka"), "ha"),
            P(("pb", "ka"), "ha"),
            P(("pb", "ka"), "ha"),
            P(),
        ),
        out_specs=(P(("pb", "ka"), "ha"), P(("pb", "ka"), "ha"), P(("pb", "ka"), "ha")),
        check_vma=False,
    )
```

```python
import functools
import math

import jax
import jax.numpy as jnp
from jax import lax
from jax.experimental import pallas as pl
from jax.experimental.pallas import tpu as pltpu
from jax.sharding import PartitionSpec as P


def block_length(row_total):
    length = row_total
    while length > 512 and length % 2 == 0:
        length = length // 2
    return length


def tile_grads(
    query_blk, grad_blk, lse_blk, delta_blk, query_pos, key_blk, value_blk, key_pos, factor
):
    scores = (
        jnp.einsum("qhd,khd->hqk", query_blk, key_blk, preferred_element_type=jnp.float32) * factor
    )
    visible = key_pos[None, :] <= query_pos[:, None]
    probs = jnp.where(visible[None], jnp.exp(scores - lse_blk.T[:, :, None]), 0.0)
    probs_low = probs.astype(jnp.bfloat16)
    value_part = jnp.einsum("hqk,qhd->khd", probs_low, grad_blk, preferred_element_type=jnp.float32)
    dprobs = jnp.einsum("qhd,khd->hqk", grad_blk, value_blk, preferred_element_type=jnp.float32)
    dscores = (probs * (dprobs - delta_blk.T[:, :, None])).astype(jnp.bfloat16)
    query_part = jnp.einsum("hqk,khd->qhd", dscores, key_blk, preferred_element_type=jnp.float32)
    key_part = jnp.einsum("hqk,qhd->khd", dscores, query_blk, preferred_element_type=jnp.float32)
    return (query_part, key_part, value_part)


def add_rows(target, update, first_row):
    length = update.shape[0]
    current = lax.dynamic_slice_in_dim(target, first_row, length, 0)
    return lax.dynamic_update_slice_in_dim(target, current + update, first_row, 0)


def body(queries, key_rows, value_rows, outputs, out_grad, saved_lse, fold_map):
    row_count, full_width = queries.shape
    head_count = saved_lse.shape[1]
    head_dim = full_width // head_count
    factor = 1.0 / math.sqrt(head_dim)
    fold_rows = row_count // 2
    size_pb = lax.axis_size("pb")
    size_ka = lax.axis_size("ka")
    index_pb = lax.axis_index("pb")
    index_ka = lax.axis_index("ka")
    key_all, value_all = (
        lax.all_gather(key_rows, "pb", axis=0, tiled=True),
        lax.all_gather(value_rows, "pb", axis=0, tiled=True),
    )
    key_len = size_pb * row_count
    key_all = key_all.reshape(key_len, head_count, head_dim)
    value_all = value_all.reshape(key_len, head_count, head_dim)
    key_iota = jnp.arange(key_len, dtype=jnp.int32)
    key_global = (key_iota // row_count * size_ka + index_ka) * row_count + key_iota % row_count
    key_pos = fold_map[key_global // fold_rows] * fold_rows + key_global % fold_rows
    query_len = size_ka * row_count
    query_first = index_pb * query_len
    query_empty = jnp.zeros((query_len, head_count, head_dim), jnp.float32)
    key_empty = jnp.zeros((key_len, head_count, head_dim), jnp.float32)
    init = (query_empty, key_empty, key_empty)
    query_src = lax.all_gather(queries, "ka", axis=0, tiled=True)
    grad_src = lax.all_gather(out_grad, "ka", axis=0, tiled=True)
    saved_src = lax.all_gather(outputs, "ka", axis=0, tiled=True)
    lse_src = lax.all_gather(saved_lse, "ka", axis=0, tiled=True)
    piece_rows = query_src.shape[0]
    step_rows = block_length(piece_rows)

    def one_block(number, state):
        dq_all, dk_all, dv_all = state
        offset = number * step_rows
        query_blk = lax.dynamic_slice_in_dim(query_src, offset, step_rows, 0).reshape(
            step_rows, head_count, head_dim
        )
        grad_blk = lax.dynamic_slice_in_dim(grad_src, offset, step_rows, 0).reshape(
            step_rows, head_count, head_dim
        )
        lse_blk = lax.dynamic_slice_in_dim(lse_src, offset, step_rows, 0).astype(jnp.float32)
        saved_blk = lax.dynamic_slice_in_dim(saved_src, offset, step_rows, 0).reshape(
            step_rows, head_count, head_dim
        )
        delta_low = jnp.einsum(
            "qhd,qhd->qh", grad_blk, saved_blk, preferred_element_type=jnp.float32
        ).astype(jnp.bfloat16)
        delta_blk = lax.optimization_barrier(delta_low).astype(jnp.float32)
        row_global = query_first + offset + jnp.arange(step_rows, dtype=jnp.int32)
        query_pos = fold_map[row_global // fold_rows] * fold_rows + row_global % fold_rows
        dq_blk, dk_part, dv_part = tile_grads(
            query_blk, grad_blk, lse_blk, delta_blk, query_pos, key_all, value_all, key_pos, factor
        )
        dk_all = dk_all + dk_part
        dv_all = dv_all + dv_part
        dq_all = add_rows(dq_all, dq_blk, offset)
        return (dq_all, dk_all, dv_all)

    dq_all, dk_all, dv_all = lax.fori_loop(0, piece_rows // step_rows, one_block, init)
    query_mine = lax.psum_scatter(
        dq_all.reshape(query_len, full_width), "ka", scatter_dimension=0, tiled=True
    )
    query_grad = (query_mine * factor).astype(jnp.bfloat16)
    key_flat = dk_all.reshape(key_len, full_width)
    value_flat = dv_all.reshape(key_len, full_width)
    key_total, value_total = lax.psum((key_flat, value_flat), "pb")
    key_mine = lax.dynamic_slice_in_dim(key_total, index_pb * row_count, row_count, 0)
    value_mine = lax.dynamic_slice_in_dim(value_total, index_pb * row_count, row_count, 0)
    key_grad = (key_mine * factor).astype(jnp.bfloat16)
    value_grad = value_mine.astype(jnp.bfloat16)
    return (query_grad, key_grad, value_grad)


MESH = pl.DeviceIdType.MESH
NT = (((1,), (1,)), ((), ()))
TN = (((0,), (0,)), ((), ()))


def plane_kernel(
    rows, factor,
    q_in, k_in, v_in, o_in, g_in, lse_in, map_in,
    dq_out, dk_out, dv_out,
    q_buf, g_buf, k_buf, v_buf, o_buf, lse_buf, map_buf, stat,
    dq_acc, dk_acc, dv_acc,
    kv_send, kv_recv, dq_send, dq_recv,
    stage, store_sem, local_sem, send_sem, recv_sem,
):
    p = lax.axis_index("pb")
    x = lax.axis_index("ka")
    h = lax.axis_index("ha")
    c = lax.rem(p, 2)
    y = p // 2
    p_core = p + 1 - 2 * c
    p_far = lax.rem(p + 2, 4)
    to_core = (p_core, x, h)
    to_x = (p, 1 - x, h)
    to_y = (p_far, x, h)
    to_both = (p_core, 1 - x, h)
    fold_rows = rows // 2

    def part(slot):
        return pl.ds(slot * rows, rows)

    locals_ = []
    for n, (src, dst) in enumerate((
        (g_in, g_buf.at[part(0)]), (o_in, o_buf), (lse_in, lse_buf), (q_in, q_buf.at[part(0)]),
        (k_in, k_buf.at[part(0)]), (v_in, v_buf.at[part(0)]), (map_in, map_buf),
    )):
        copy = pltpu.make_async_copy(src, dst, local_sem.at[n])
        copy.start()
        locals_.append(copy)

    barrier = pltpu.get_barrier_semaphore()
    for peer in (to_core, to_x, to_y, to_both):
        pl.semaphore_signal(barrier, inc=1, device_id=peer, device_id_type=MESH)
    pl.semaphore_wait(barrier, 4)

    sends = []

    def send(n, src, dst, peer):
        copy = pltpu.make_async_remote_copy(
            src_ref=src, dst_ref=dst, send_sem=send_sem.at[n], recv_sem=recv_sem.at[n],
            device_id=peer, device_id_type=MESH,
        )
        copy.start()
        sends.append(copy)
        return copy

    q_x = send(0, q_in, q_buf.at[part(2)], to_x)
    k_y = send(1, k_in, k_buf.at[part(1)], to_y)
    q_c = send(2, q_in, q_buf.at[part(1)], to_core)
    g_c = send(3, g_in, g_buf.at[part(1)], to_core)
    g_x = send(4, g_in, g_buf.at[part(2)], to_x)
    v_y = send(5, v_in, v_buf.at[part(1)], to_y)

    for copy in locals_[:3]:
        copy.wait()
    gram = lax.dot_general(o_buf[...], g_buf[part(0)], NT, preferred_element_type=jnp.float32)
    down = lax.broadcasted_iota(jnp.int32, (rows, rows), 0)
    along = lax.broadcasted_iota(jnp.int32, (rows, rows), 1)
    delta = jnp.sum(jnp.where(down == along, gram, 0.0), axis=0, keepdims=True)
    delta = delta.astype(jnp.bfloat16).astype(jnp.float32)
    log2e = math.log2(math.e)
    lse = lse_buf[...].astype(jnp.float32) * log2e
    which = lax.broadcasted_iota(jnp.int32, (8, rows), 0)
    stat[0] = jnp.where(which == 0, lse, delta)
    st_c = send(6, stat.at[0], stat.at[1], to_core)
    st_x = send(7, stat.at[0], stat.at[2], to_x)
    st_b = send(8, stat.at[0], stat.at[3], to_both)
    for copy in locals_[3:]:
        copy.wait()

    q_owner = (p * 2 + x, p_core * 2 + x, p * 2 + 1 - x, p_core * 2 + 1 - x)
    k_owner = (p * 2 + x, p_far * 2 + x)
    half = lax.broadcasted_iota(jnp.int32, (1, rows), 1) // fold_rows
    lane = lax.broadcasted_iota(jnp.int32, (fold_rows, rows), 1) % fold_rows
    level = lax.broadcasted_iota(jnp.int32, (fold_rows, rows), 0)

    def probabilities(j, s, scores):
        q_fold = jnp.where(half == 0, map_buf[q_owner[s] * 2], map_buf[q_owner[s] * 2 + 1])
        lse_row = stat[s, 0:1, :]
        parts = []
        for i in range(2):
            k_fold = map_buf[k_owner[j] * 2 + i]
            scaled = scores[i * fold_rows:(i + 1) * fold_rows] * (factor * log2e)
            if j == 0 and s == 0:
                seen = k_fold * fold_rows + level <= q_fold * fold_rows + lane
                parts.append(jnp.where(seen, jnp.exp2(scaled - lse_row), 0.0))
            else:
                parts.append(jnp.exp2(scaled - jnp.where(q_fold > k_fold, lse_row, 1e30)))
        return jnp.concatenate(parts, axis=0)

    def tile(j, s, first_q, first_k, after_dv=None):
        keys, values = k_buf[part(j)], v_buf[part(j)]
        query, grad = q_buf[part(s)], g_buf[part(s)]
        scores = lax.dot_general(keys, query, NT, preferred_element_type=jnp.float32)
        dprobs = lax.dot_general(values, grad, NT, preferred_element_type=jnp.float32)
        probs = probabilities(j, s, scores)
        dv = jnp.dot(probs.astype(jnp.bfloat16), grad, preferred_element_type=jnp.float32)
        dv_acc[part(j)] = dv if first_k else dv_acc[part(j)] + dv
        if after_dv is not None:
            after_dv()
        dscores = (probs * (dprobs - stat[s, 1:2, :])).astype(jnp.bfloat16)
        dk = jnp.dot(dscores, query, preferred_element_type=jnp.float32)
        dk_acc[part(j)] = dk if first_k else dk_acc[part(j)] + dk
        dq = lax.dot_general(dscores, keys, TN, preferred_element_type=jnp.float32)
        dq_acc[part(s)] = dq if first_q else dq_acc[part(s)] + dq

    def send_dq(n, s, peer):
        dq_send[s - 1] = dq_acc[part(s)].astype(jnp.bfloat16)
        return send(n, dq_send.at[s - 1], dq_recv.at[s - 1], peer)

    def send_kv(n, i, acc):
        kv_send[i] = acc[part(1)].astype(jnp.bfloat16)
        return send(n, kv_send.at[i], kv_recv.at[i], to_y)

    stores = []

    def store(n, dst):
        copy = pltpu.make_async_copy(stage.at[n], dst, store_sem.at[n])
        copy.start()
        stores.append(copy)

    tile(0, 0, True, True)
    q_c.wait_recv()
    g_c.wait_recv()
    st_c.wait_recv()
    tile(0, 1, True, False)
    q_x.wait_recv()
    q_r = send(9, q_buf.at[part(2)], q_buf.at[part(3)], to_core)
    k_y.wait_recv()
    g_x.wait_recv()
    g_r = send(10, g_buf.at[part(2)], g_buf.at[part(3)], to_core)
    v_y.wait_recv()
    tile(1, 0, False, True)
    tile(1, 1, False, False)
    dq_1 = send_dq(11, 1, to_core)
    st_x.wait_recv()
    tile(1, 2, True, False)
    tile(0, 2, False, False)
    dq_2 = send_dq(12, 2, to_x)
    q_r.wait_recv()
    g_r.wait_recv()
    st_b.wait_recv()
    late = []
    tile(1, 3, True, False, lambda: late.append(send_kv(13, 0, dv_acc)))
    late.append(send_kv(14, 1, dk_acc))
    tile(0, 3, False, False)
    dq_3 = send_dq(15, 3, to_both)
    dq_1.wait_recv()
    dq_2.wait_recv()
    dq_mine = (dq_acc[part(0)] + dq_recv[0].astype(jnp.float32)) + dq_recv[1].astype(jnp.float32)
    late[0].wait_recv()
    stage[2] = (dv_acc[part(0)] + kv_recv[0].astype(jnp.float32)).astype(jnp.bfloat16)
    store(2, dv_out)
    late[1].wait_recv()
    stage[1] = (
        (dk_acc[part(0)] + kv_recv[1].astype(jnp.float32)) * factor).astype(jnp.bfloat16)
    store(1, dk_out)
    dq_3.wait_recv()
    stage[0] = ((dq_mine + dq_recv[2].astype(jnp.float32)) * factor).astype(jnp.bfloat16)
    store(0, dq_out)
    for copy in sends:
        copy.wait_send()
    for copy in stores:
        copy.wait()


def store_kernel(dq_in, dk_in, dv_in, dq_out, dk_out, dv_out, sems):
    copies = []
    for n, (src, dst) in enumerate(((dq_in, dq_out), (dk_in, dk_out), (dv_in, dv_out))):
        copy = pltpu.make_async_copy(src, dst, sems.at[n])
        copy.start()
        copies.append(copy)
    for copy in copies:
        copy.wait()


def plane_body(queries, key_rows, value_rows, outputs, out_grad, saved_lse, fold_map):
    rows, width = queries.shape
    factor = 1.0 / math.sqrt(width)
    low, full = jnp.bfloat16, jnp.float32
    grad = jax.ShapeDtypeStruct((rows, width), low)
    grads = pl.pallas_call(
        functools.partial(plane_kernel, rows, factor),
        out_shape=(grad, grad, grad),
        in_specs=[pl.BlockSpec(memory_space=pl.ANY)] * 7,
        out_specs=[pl.BlockSpec(memory_space=pl.ANY)] * 3,
        scratch_shapes=[
            pltpu.VMEM((4 * rows, width), low),
            pltpu.VMEM((4 * rows, width), low),
            pltpu.VMEM((2 * rows, width), low),
            pltpu.VMEM((2 * rows, width), low),
            pltpu.VMEM((rows, width), low),
            pltpu.VMEM((1, rows), low),
            pltpu.SMEM(fold_map.shape, jnp.int32),
            pltpu.VMEM((4, 8, rows), full),
            pltpu.VMEM((4 * rows, width), full),
            pltpu.VMEM((2 * rows, width), full),
            pltpu.VMEM((2 * rows, width), full),
            pltpu.VMEM((2, rows, width), low),
            pltpu.VMEM((2, rows, width), low),
            pltpu.VMEM((3, rows, width), low),
            pltpu.VMEM((3, rows, width), low),
            pltpu.VMEM((3, rows, width), low),
            pltpu.SemaphoreType.DMA((3,)),
            pltpu.SemaphoreType.DMA((7,)),
            pltpu.SemaphoreType.DMA((16,)),
            pltpu.SemaphoreType.DMA((16,)),
        ],
        compiler_params=pltpu.CompilerParams(
            collective_id=0, has_side_effects=True, vmem_limit_bytes=60 * 2**20
        ),
        cost_estimate=pl.CostEstimate(
            flops=80 * rows * rows * width,
            bytes_accessed=16 * rows * width,
            transcendentals=8 * rows * rows,
        ),
    )(queries, key_rows, value_rows, outputs, out_grad, saved_lse.reshape(1, rows), fold_map)
    return pl.pallas_call(
        store_kernel,
        out_shape=(grad, grad, grad),
        in_specs=[pl.BlockSpec(memory_space=pl.ANY)] * 3,
        out_specs=[pl.BlockSpec(memory_space=pl.ANY)] * 3,
        scratch_shapes=[pltpu.SemaphoreType.DMA((3,))],
        compiler_params=pltpu.CompilerParams(vmem_limit_bytes=60 * 2**20),
    )(*grads)


def solution(mesh):
    plane = mesh.shape["pb"] == 4 and mesh.shape["ka"] == 2
    return jax.shard_map(
        plane_body if plane else body,
        mesh=mesh,
        in_specs=(
            P(("pb", "ka"), "ha"),
            P(("pb", "ka"), "ha"),
            P(("pb", "ka"), "ha"),
            P(("pb", "ka"), "ha"),
            P(("pb", "ka"), "ha"),
            P(("pb", "ka"), "ha"),
            P(),
        ),
        out_specs=(P(("pb", "ka"), "ha"), P(("pb", "ka"), "ha"), P(("pb", "ka"), "ha")),
        check_vma=False,
    )
```

```python
import functools
import math

import jax
import jax.numpy as jnp
from jax import lax
from jax.experimental import pallas as pl
from jax.experimental.pallas import tpu as pltpu
from jax.sharding import PartitionSpec as P


def block_length(row_total):
    length = row_total
    while length > 512 and length % 2 == 0:
        length = length // 2
    return length


def tile_grads(
    query_blk, grad_blk, lse_blk, delta_blk, query_pos, key_blk, value_blk, key_pos, factor
):
    scores = (
        jnp.einsum("qhd,khd->hqk", query_blk, key_blk, preferred_element_type=jnp.float32) * factor
    )
    visible = key_pos[None, :] <= query_pos[:, None]
    probs = jnp.where(visible[None], jnp.exp(scores - lse_blk.T[:, :, None]), 0.0)
    probs_low = probs.astype(jnp.bfloat16)
    value_part = jnp.einsum("hqk,qhd->khd", probs_low, grad_blk, preferred_element_type=jnp.float32)
    dprobs = jnp.einsum("qhd,khd->hqk", grad_blk, value_blk, preferred_element_type=jnp.float32)
    dscores = (probs * (dprobs - delta_blk.T[:, :, None])).astype(jnp.bfloat16)
    query_part = jnp.einsum("hqk,khd->qhd", dscores, key_blk, preferred_element_type=jnp.float32)
    key_part = jnp.einsum("hqk,qhd->khd", dscores, query_blk, preferred_element_type=jnp.float32)
    return (query_part, key_part, value_part)


def add_rows(target, update, first_row):
    length = update.shape[0]
    current = lax.dynamic_slice_in_dim(target, first_row, length, 0)
    return lax.dynamic_update_slice_in_dim(target, current + update, first_row, 0)


def body(queries, key_rows, value_rows, outputs, out_grad, saved_lse, fold_map):
    row_count, full_width = queries.shape
    head_count = saved_lse.shape[1]
    head_dim = full_width // head_count
    factor = 1.0 / math.sqrt(head_dim)
    fold_rows = row_count // 2
    size_pb = lax.axis_size("pb")
    size_ka = lax.axis_size("ka")
    index_pb = lax.axis_index("pb")
    index_ka = lax.axis_index("ka")
    key_all, value_all = (
        lax.all_gather(key_rows, "pb", axis=0, tiled=True),
        lax.all_gather(value_rows, "pb", axis=0, tiled=True),
    )
    key_len = size_pb * row_count
    key_all = key_all.reshape(key_len, head_count, head_dim)
    value_all = value_all.reshape(key_len, head_count, head_dim)
    key_iota = jnp.arange(key_len, dtype=jnp.int32)
    key_global = (key_iota // row_count * size_ka + index_ka) * row_count + key_iota % row_count
    key_pos = fold_map[key_global // fold_rows] * fold_rows + key_global % fold_rows
    query_len = size_ka * row_count
    query_first = index_pb * query_len
    query_empty = jnp.zeros((query_len, head_count, head_dim), jnp.float32)
    key_empty = jnp.zeros((key_len, head_count, head_dim), jnp.float32)
    init = (query_empty, key_empty, key_empty)
    query_src = lax.all_gather(queries, "ka", axis=0, tiled=True)
    grad_src = lax.all_gather(out_grad, "ka", axis=0, tiled=True)
    saved_src = lax.all_gather(outputs, "ka", axis=0, tiled=True)
    lse_src = lax.all_gather(saved_lse, "ka", axis=0, tiled=True)
    piece_rows = query_src.shape[0]
    step_rows = block_length(piece_rows)

    def one_block(number, state):
        dq_all, dk_all, dv_all = state
        offset = number * step_rows
        query_blk = lax.dynamic_slice_in_dim(query_src, offset, step_rows, 0).reshape(
            step_rows, head_count, head_dim
        )
        grad_blk = lax.dynamic_slice_in_dim(grad_src, offset, step_rows, 0).reshape(
            step_rows, head_count, head_dim
        )
        lse_blk = lax.dynamic_slice_in_dim(lse_src, offset, step_rows, 0).astype(jnp.float32)
        saved_blk = lax.dynamic_slice_in_dim(saved_src, offset, step_rows, 0).reshape(
            step_rows, head_count, head_dim
        )
        delta_low = jnp.einsum(
            "qhd,qhd->qh", grad_blk, saved_blk, preferred_element_type=jnp.float32
        ).astype(jnp.bfloat16)
        delta_blk = lax.optimization_barrier(delta_low).astype(jnp.float32)
        row_global = query_first + offset + jnp.arange(step_rows, dtype=jnp.int32)
        query_pos = fold_map[row_global // fold_rows] * fold_rows + row_global % fold_rows
        dq_blk, dk_part, dv_part = tile_grads(
            query_blk, grad_blk, lse_blk, delta_blk, query_pos, key_all, value_all, key_pos, factor
        )
        dk_all = dk_all + dk_part
        dv_all = dv_all + dv_part
        dq_all = add_rows(dq_all, dq_blk, offset)
        return (dq_all, dk_all, dv_all)

    dq_all, dk_all, dv_all = lax.fori_loop(0, piece_rows // step_rows, one_block, init)
    query_mine = lax.psum_scatter(
        dq_all.reshape(query_len, full_width), "ka", scatter_dimension=0, tiled=True
    )
    query_grad = (query_mine * factor).astype(jnp.bfloat16)
    key_flat = dk_all.reshape(key_len, full_width)
    value_flat = dv_all.reshape(key_len, full_width)
    key_total, value_total = lax.psum((key_flat, value_flat), "pb")
    key_mine = lax.dynamic_slice_in_dim(key_total, index_pb * row_count, row_count, 0)
    value_mine = lax.dynamic_slice_in_dim(value_total, index_pb * row_count, row_count, 0)
    key_grad = (key_mine * factor).astype(jnp.bfloat16)
    value_grad = value_mine.astype(jnp.bfloat16)
    return (query_grad, key_grad, value_grad)


MESH = pl.DeviceIdType.MESH
NT = (((1,), (1,)), ((), ()))
TN = (((0,), (0,)), ((), ()))


def plane_kernel(
    rows, factor,
    q_in, k_in, v_in, o_in, g_in, lse_in, map_in,
    dq_out, dk_out, dv_out,
    q_buf, g_buf, k_buf, v_buf, o_buf, lse_buf, map_buf, stat,
    dq_acc, dk_acc, dv_acc,
    kv_send, kv_recv, dq_send, dq_recv,
    local_sem, send_sem, recv_sem,
):
    p = lax.axis_index("pb")
    x = lax.axis_index("ka")
    h = lax.axis_index("ha")
    c = lax.rem(p, 2)
    y = p // 2
    p_core = p + 1 - 2 * c
    p_far = lax.rem(p + 2, 4)
    to_core = (p_core, x, h)
    to_x = (p, 1 - x, h)
    to_y = (p_far, x, h)
    to_both = (p_core, 1 - x, h)
    fold_rows = rows // 2

    def part(slot):
        return pl.ds(slot * rows, rows)

    locals_ = []
    for n, (src, dst) in enumerate((
        (g_in, g_buf.at[part(0)]), (o_in, o_buf), (lse_in, lse_buf), (q_in, q_buf.at[part(0)]),
        (k_in, k_buf.at[part(0)]), (v_in, v_buf.at[part(0)]), (map_in, map_buf),
    )):
        copy = pltpu.make_async_copy(src, dst, local_sem.at[n])
        copy.start()
        locals_.append(copy)

    barrier = pltpu.get_barrier_semaphore()
    for peer in (to_core, to_x, to_y, to_both):
        pl.semaphore_signal(barrier, inc=1, device_id=peer, device_id_type=MESH)
    pl.semaphore_wait(barrier, 4)

    sends = []

    def send(n, src, dst, peer):
        copy = pltpu.make_async_remote_copy(
            src_ref=src, dst_ref=dst, send_sem=send_sem.at[n], recv_sem=recv_sem.at[n],
            device_id=peer, device_id_type=MESH,
        )
        copy.start()
        sends.append(copy)
        return copy

    q_x = send(0, q_in, q_buf.at[part(2)], to_x)
    k_y = send(1, k_in, k_buf.at[part(1)], to_y)
    q_c = send(2, q_in, q_buf.at[part(1)], to_core)
    g_c = send(3, g_in, g_buf.at[part(1)], to_core)
    g_x = send(4, g_in, g_buf.at[part(2)], to_x)
    v_y = send(5, v_in, v_buf.at[part(1)], to_y)

    for copy in locals_[:3]:
        copy.wait()
    gram = lax.dot_general(o_buf[...], g_buf[part(0)], NT, preferred_element_type=jnp.float32)
    down = lax.broadcasted_iota(jnp.int32, (rows, rows), 0)
    along = lax.broadcasted_iota(jnp.int32, (rows, rows), 1)
    delta = jnp.sum(jnp.where(down == along, gram, 0.0), axis=0, keepdims=True)
    delta = delta.astype(jnp.bfloat16).astype(jnp.float32)
    log2e = math.log2(math.e)
    lse = lse_buf[...].astype(jnp.float32) * log2e
    which = lax.broadcasted_iota(jnp.int32, (8, rows), 0)
    stat[0] = jnp.where(which == 0, lse, delta)
    st_c = send(6, stat.at[0], stat.at[1], to_core)
    st_x = send(7, stat.at[0], stat.at[2], to_x)
    st_b = send(8, stat.at[0], stat.at[3], to_both)
    for copy in locals_[3:]:
        copy.wait()

    q_owner = (p * 2 + x, p_core * 2 + x, p * 2 + 1 - x, p_core * 2 + 1 - x)
    k_owner = (p * 2 + x, p_far * 2 + x)
    half = lax.broadcasted_iota(jnp.int32, (1, rows), 1) // fold_rows
    lane = lax.broadcasted_iota(jnp.int32, (fold_rows, rows), 1) % fold_rows
    level = lax.broadcasted_iota(jnp.int32, (fold_rows, rows), 0)

    def probabilities(j, s, scores):
        q_fold = jnp.where(half == 0, map_buf[q_owner[s] * 2], map_buf[q_owner[s] * 2 + 1])
        lse_row = stat[s, 0:1, :]
        parts = []
        for i in range(2):
            k_fold = map_buf[k_owner[j] * 2 + i]
            scaled = scores[i * fold_rows:(i + 1) * fold_rows] * (factor * log2e)
            if j == 0 and s == 0:
                seen = k_fold * fold_rows + level <= q_fold * fold_rows + lane
                parts.append(jnp.where(seen, jnp.exp2(scaled - lse_row), 0.0))
            else:
                parts.append(jnp.exp2(scaled - jnp.where(q_fold > k_fold, lse_row, 1e30)))
        return jnp.concatenate(parts, axis=0)

    def tile(j, s, first_q, first_k, after_dv=None):
        keys, values = k_buf[part(j)], v_buf[part(j)]
        query, grad = q_buf[part(s)], g_buf[part(s)]
        scores = lax.dot_general(keys, query, NT, preferred_element_type=jnp.float32)
        dprobs = lax.dot_general(values, grad, NT, preferred_element_type=jnp.float32)
        probs = probabilities(j, s, scores)
        dv = jnp.dot(probs.astype(jnp.bfloat16), grad, preferred_element_type=jnp.float32)
        dv_acc[part(j)] = dv if first_k else dv_acc[part(j)] + dv
        if after_dv is not None:
            after_dv()
        dscores = (probs * (dprobs - stat[s, 1:2, :])).astype(jnp.bfloat16)
        dk = jnp.dot(dscores, query, preferred_element_type=jnp.float32)
        dk_acc[part(j)] = dk if first_k else dk_acc[part(j)] + dk
        dq = lax.dot_general(dscores, keys, TN, preferred_element_type=jnp.float32)
        dq_acc[part(s)] = dq if first_q else dq_acc[part(s)] + dq

    def send_dq(n, s, peer):
        dq_send[s - 1] = dq_acc[part(s)].astype(jnp.bfloat16)
        return send(n, dq_send.at[s - 1], dq_recv.at[s - 1], peer)

    def send_kv(n, i, acc):
        kv_send[i] = acc[part(1)].astype(jnp.bfloat16)
        return send(n, kv_send.at[i], kv_recv.at[i], to_y)

    tile(0, 0, True, True)
    q_c.wait_recv()
    g_c.wait_recv()
    st_c.wait_recv()
    tile(0, 1, True, False)
    q_x.wait_recv()
    q_r = send(9, q_buf.at[part(2)], q_buf.at[part(3)], to_core)
    k_y.wait_recv()
    g_x.wait_recv()
    g_r = send(10, g_buf.at[part(2)], g_buf.at[part(3)], to_core)
    v_y.wait_recv()
    tile(1, 0, False, True)
    tile(1, 1, False, False)
    dq_1 = send_dq(11, 1, to_core)
    st_x.wait_recv()
    tile(1, 2, True, False)
    tile(0, 2, False, False)
    dq_2 = send_dq(12, 2, to_x)
    q_r.wait_recv()
    g_r.wait_recv()
    st_b.wait_recv()
    late = []
    tile(1, 3, True, False, lambda: late.append(send_kv(13, 0, dv_acc)))
    late.append(send_kv(14, 1, dk_acc))
    tile(0, 3, False, False)
    dq_3 = send_dq(15, 3, to_both)
    dq_1.wait_recv()
    dq_2.wait_recv()
    dq_mine = (dq_acc[part(0)] + dq_recv[0].astype(jnp.float32)) + dq_recv[1].astype(jnp.float32)
    late[0].wait_recv()
    dv_out[...] = (dv_acc[part(0)] + kv_recv[0].astype(jnp.float32)).astype(jnp.bfloat16)
    late[1].wait_recv()
    dk_out[...] = (
        (dk_acc[part(0)] + kv_recv[1].astype(jnp.float32)) * factor).astype(jnp.bfloat16)
    dq_3.wait_recv()
    dq_out[...] = ((dq_mine + dq_recv[2].astype(jnp.float32)) * factor).astype(jnp.bfloat16)
    for copy in sends:
        copy.wait_send()


def store_kernel(dq_in, dk_in, dv_in, dq_out, dk_out, dv_out, sems):
    copies = []
    for n, (src, dst) in enumerate(((dq_in, dq_out), (dk_in, dk_out), (dv_in, dv_out))):
        copy = pltpu.make_async_copy(src, dst, sems.at[n])
        copy.start()
        copies.append(copy)
    for copy in copies:
        copy.wait()


def plane_body(queries, key_rows, value_rows, outputs, out_grad, saved_lse, fold_map):
    rows, width = queries.shape
    factor = 1.0 / math.sqrt(width)
    low, full = jnp.bfloat16, jnp.float32
    grad = jax.ShapeDtypeStruct((rows, width), low)
    arrays = [
        pltpu.with_memory_space_constraint(a, pltpu.HBM)
        for a in (queries, key_rows, value_rows, outputs, out_grad, saved_lse.reshape(1, rows),
                  fold_map)
    ]
    grads = pl.pallas_call(
        functools.partial(plane_kernel, rows, factor),
        out_shape=(pltpu.VMEM((rows, width), low),) * 3,
        in_specs=[pl.BlockSpec(memory_space=pl.ANY)] * 7,
        out_specs=[pl.BlockSpec(memory_space=pltpu.VMEM)] * 3,
        scratch_shapes=[
            pltpu.VMEM((4 * rows, width), low),
            pltpu.VMEM((4 * rows, width), low),
            pltpu.VMEM((2 * rows, width), low),
            pltpu.VMEM((2 * rows, width), low),
            pltpu.VMEM((rows, width), low),
            pltpu.VMEM((1, rows), low),
            pltpu.SMEM(fold_map.shape, jnp.int32),
            pltpu.VMEM((4, 8, rows), full),
            pltpu.VMEM((4 * rows, width), full),
            pltpu.VMEM((2 * rows, width), full),
            pltpu.VMEM((2 * rows, width), full),
            pltpu.VMEM((2, rows, width), low),
            pltpu.VMEM((2, rows, width), low),
            pltpu.VMEM((3, rows, width), low),
            pltpu.VMEM((3, rows, width), low),
            pltpu.SemaphoreType.DMA((7,)),
            pltpu.SemaphoreType.DMA((16,)),
            pltpu.SemaphoreType.DMA((16,)),
        ],
        compiler_params=pltpu.CompilerParams(
            collective_id=0, has_side_effects=True, vmem_limit_bytes=32 * 2**20
        ),
        cost_estimate=pl.CostEstimate(
            flops=80 * rows * rows * width,
            bytes_accessed=16 * rows * width,
            transcendentals=8 * rows * rows,
        ),
    )(*arrays)
    return pl.pallas_call(
        store_kernel,
        out_shape=(grad, grad, grad),
        in_specs=[pl.BlockSpec(memory_space=pl.ANY)] * 3,
        out_specs=[pl.BlockSpec(memory_space=pl.ANY)] * 3,
        scratch_shapes=[pltpu.SemaphoreType.DMA((3,))],
    )(*grads)


def solution(mesh):
    plane = mesh.shape["pb"] == 4 and mesh.shape["ka"] == 2
    return jax.shard_map(
        plane_body if plane else body,
        mesh=mesh,
        in_specs=(
            P(("pb", "ka"), "ha"),
            P(("pb", "ka"), "ha"),
            P(("pb", "ka"), "ha"),
            P(("pb", "ka"), "ha"),
            P(("pb", "ka"), "ha"),
            P(("pb", "ka"), "ha"),
            P(),
        ),
        out_specs=(P(("pb", "ka"), "ha"), P(("pb", "ka"), "ha"), P(("pb", "ka"), "ha")),
        check_vma=False,
    )
```

```python
import functools
import math

import jax
import jax.numpy as jnp
from jax import lax
from jax.experimental import pallas as pl
from jax.experimental.pallas import tpu as pltpu
from jax.sharding import PartitionSpec as P


def block_length(row_total):
    length = row_total
    while length > 512 and length % 2 == 0:
        length = length // 2
    return length


def tile_grads(
    query_blk, grad_blk, lse_blk, delta_blk, query_pos, key_blk, value_blk, key_pos, factor
):
    scores = (
        jnp.einsum("qhd,khd->hqk", query_blk, key_blk, preferred_element_type=jnp.float32) * factor
    )
    visible = key_pos[None, :] <= query_pos[:, None]
    probs = jnp.where(visible[None], jnp.exp(scores - lse_blk.T[:, :, None]), 0.0)
    probs_low = probs.astype(jnp.bfloat16)
    value_part = jnp.einsum("hqk,qhd->khd", probs_low, grad_blk, preferred_element_type=jnp.float32)
    dprobs = jnp.einsum("qhd,khd->hqk", grad_blk, value_blk, preferred_element_type=jnp.float32)
    dscores = (probs * (dprobs - delta_blk.T[:, :, None])).astype(jnp.bfloat16)
    query_part = jnp.einsum("hqk,khd->qhd", dscores, key_blk, preferred_element_type=jnp.float32)
    key_part = jnp.einsum("hqk,qhd->khd", dscores, query_blk, preferred_element_type=jnp.float32)
    return (query_part, key_part, value_part)


def add_rows(target, update, first_row):
    length = update.shape[0]
    current = lax.dynamic_slice_in_dim(target, first_row, length, 0)
    return lax.dynamic_update_slice_in_dim(target, current + update, first_row, 0)


def body(queries, key_rows, value_rows, outputs, out_grad, saved_lse, fold_map):
    row_count, full_width = queries.shape
    head_count = saved_lse.shape[1]
    head_dim = full_width // head_count
    factor = 1.0 / math.sqrt(head_dim)
    fold_rows = row_count // 2
    size_pb = lax.axis_size("pb")
    size_ka = lax.axis_size("ka")
    index_pb = lax.axis_index("pb")
    index_ka = lax.axis_index("ka")
    key_all, value_all = (
        lax.all_gather(key_rows, "pb", axis=0, tiled=True),
        lax.all_gather(value_rows, "pb", axis=0, tiled=True),
    )
    key_len = size_pb * row_count
    key_all = key_all.reshape(key_len, head_count, head_dim)
    value_all = value_all.reshape(key_len, head_count, head_dim)
    key_iota = jnp.arange(key_len, dtype=jnp.int32)
    key_global = (key_iota // row_count * size_ka + index_ka) * row_count + key_iota % row_count
    key_pos = fold_map[key_global // fold_rows] * fold_rows + key_global % fold_rows
    query_len = size_ka * row_count
    query_first = index_pb * query_len
    query_empty = jnp.zeros((query_len, head_count, head_dim), jnp.float32)
    key_empty = jnp.zeros((key_len, head_count, head_dim), jnp.float32)
    init = (query_empty, key_empty, key_empty)
    query_src = lax.all_gather(queries, "ka", axis=0, tiled=True)
    grad_src = lax.all_gather(out_grad, "ka", axis=0, tiled=True)
    saved_src = lax.all_gather(outputs, "ka", axis=0, tiled=True)
    lse_src = lax.all_gather(saved_lse, "ka", axis=0, tiled=True)
    piece_rows = query_src.shape[0]
    step_rows = block_length(piece_rows)

    def one_block(number, state):
        dq_all, dk_all, dv_all = state
        offset = number * step_rows
        query_blk = lax.dynamic_slice_in_dim(query_src, offset, step_rows, 0).reshape(
            step_rows, head_count, head_dim
        )
        grad_blk = lax.dynamic_slice_in_dim(grad_src, offset, step_rows, 0).reshape(
            step_rows, head_count, head_dim
        )
        lse_blk = lax.dynamic_slice_in_dim(lse_src, offset, step_rows, 0).astype(jnp.float32)
        saved_blk = lax.dynamic_slice_in_dim(saved_src, offset, step_rows, 0).reshape(
            step_rows, head_count, head_dim
        )
        delta_low = jnp.einsum(
            "qhd,qhd->qh", grad_blk, saved_blk, preferred_element_type=jnp.float32
        ).astype(jnp.bfloat16)
        delta_blk = lax.optimization_barrier(delta_low).astype(jnp.float32)
        row_global = query_first + offset + jnp.arange(step_rows, dtype=jnp.int32)
        query_pos = fold_map[row_global // fold_rows] * fold_rows + row_global % fold_rows
        dq_blk, dk_part, dv_part = tile_grads(
            query_blk, grad_blk, lse_blk, delta_blk, query_pos, key_all, value_all, key_pos, factor
        )
        dk_all = dk_all + dk_part
        dv_all = dv_all + dv_part
        dq_all = add_rows(dq_all, dq_blk, offset)
        return (dq_all, dk_all, dv_all)

    dq_all, dk_all, dv_all = lax.fori_loop(0, piece_rows // step_rows, one_block, init)
    query_mine = lax.psum_scatter(
        dq_all.reshape(query_len, full_width), "ka", scatter_dimension=0, tiled=True
    )
    query_grad = (query_mine * factor).astype(jnp.bfloat16)
    key_flat = dk_all.reshape(key_len, full_width)
    value_flat = dv_all.reshape(key_len, full_width)
    key_total, value_total = lax.psum((key_flat, value_flat), "pb")
    key_mine = lax.dynamic_slice_in_dim(key_total, index_pb * row_count, row_count, 0)
    value_mine = lax.dynamic_slice_in_dim(value_total, index_pb * row_count, row_count, 0)
    key_grad = (key_mine * factor).astype(jnp.bfloat16)
    value_grad = value_mine.astype(jnp.bfloat16)
    return (query_grad, key_grad, value_grad)


MESH = pl.DeviceIdType.MESH
NT = (((1,), (1,)), ((), ()))
TN = (((0,), (0,)), ((), ()))


def plane_kernel(
    rows, factor,
    q_in, k_in, v_in, o_in, g_in, lse_in, map_in,
    dq_out, dk_out, dv_out,
    q_buf, g_buf, k_buf, v_buf, o_buf, lse_buf, map_buf, stat,
    dq_acc, dk_acc, dv_acc,
    kv_send, kv_recv, dq_send, dq_recv,
    local_sem, send_sem, recv_sem,
):
    p = lax.axis_index("pb")
    x = lax.axis_index("ka")
    h = lax.axis_index("ha")
    c = lax.rem(p, 2)
    y = p // 2
    p_core = p + 1 - 2 * c
    p_far = lax.rem(p + 2, 4)
    to_core = (p_core, x, h)
    to_x = (p, 1 - x, h)
    to_y = (p_far, x, h)
    to_both = (p_core, 1 - x, h)
    fold_rows = rows // 2

    def part(slot):
        return pl.ds(slot * rows, rows)

    barrier = pltpu.get_barrier_semaphore()
    for peer in (to_core, to_x, to_y, to_both):
        pl.semaphore_signal(barrier, inc=1, device_id=peer, device_id_type=MESH)
    locals_ = []
    for n, (src, dst) in enumerate((
        (g_in, g_buf.at[part(0)]), (o_in, o_buf), (lse_in, lse_buf), (q_in, q_buf.at[part(0)]),
        (k_in, k_buf.at[part(0)]), (v_in, v_buf.at[part(0)]), (map_in, map_buf),
    )):
        copy = pltpu.make_async_copy(src, dst, local_sem.at[n])
        copy.start()
        locals_.append(copy)
    pl.semaphore_wait(barrier, 4)

    sends = []

    def send(n, src, dst, peer):
        copy = pltpu.make_async_remote_copy(
            src_ref=src, dst_ref=dst, send_sem=send_sem.at[n], recv_sem=recv_sem.at[n],
            device_id=peer, device_id_type=MESH,
        )
        copy.start()
        sends.append(copy)
        return copy

    q_x = send(0, q_in, q_buf.at[part(2)], to_x)
    k_y = send(1, k_in, k_buf.at[part(1)], to_y)
    q_c = send(2, q_in, q_buf.at[part(1)], to_core)
    g_c = send(3, g_in, g_buf.at[part(1)], to_core)
    g_x = send(4, g_in, g_buf.at[part(2)], to_x)
    v_y = send(5, v_in, v_buf.at[part(1)], to_y)

    for copy in locals_[:3]:
        copy.wait()
    gram = lax.dot_general(o_buf[...], g_buf[part(0)], NT, preferred_element_type=jnp.float32)
    down = lax.broadcasted_iota(jnp.int32, (rows, rows), 0)
    along = lax.broadcasted_iota(jnp.int32, (rows, rows), 1)
    delta = jnp.sum(jnp.where(down == along, gram, 0.0), axis=0, keepdims=True)
    delta = delta.astype(jnp.bfloat16).astype(jnp.float32)
    log2e = math.log2(math.e)
    lse = lse_buf[...].astype(jnp.float32) * log2e
    which = lax.broadcasted_iota(jnp.int32, (8, rows), 0)
    stat[0] = jnp.where(which == 0, lse, delta)
    st_c = send(6, stat.at[0], stat.at[1], to_core)
    st_x = send(7, stat.at[0], stat.at[2], to_x)
    st_b = send(8, stat.at[0], stat.at[3], to_both)
    for copy in locals_[3:]:
        copy.wait()

    q_owner = (p * 2 + x, p_core * 2 + x, p * 2 + 1 - x, p_core * 2 + 1 - x)
    k_owner = (p * 2 + x, p_far * 2 + x)
    half = lax.broadcasted_iota(jnp.int32, (1, rows), 1) // fold_rows
    lane = lax.broadcasted_iota(jnp.int32, (fold_rows, rows), 1) % fold_rows
    level = lax.broadcasted_iota(jnp.int32, (fold_rows, rows), 0)

    def span(slots):
        return pl.ds(slots[0] * rows, len(slots) * rows)

    def stat_row(n, slots):
        return jnp.concatenate([stat[s, n:n + 1, :] for s in slots], axis=1)

    def probabilities(keyed, asked, scores):
        own = keyed == [0] and asked == [0]
        q_fold = jnp.concatenate([
            jnp.where(half == 0, map_buf[q_owner[s] * 2], map_buf[q_owner[s] * 2 + 1])
            for s in asked], axis=1)
        lse_row = stat_row(0, asked)
        parts = []
        for n in range(2 * len(keyed)):
            k_fold = map_buf[k_owner[keyed[n // 2]] * 2 + n % 2]
            scaled = scores[n * fold_rows:(n + 1) * fold_rows] * (factor * log2e)
            if own:
                seen = k_fold * fold_rows + level <= q_fold * fold_rows + lane
                parts.append(jnp.where(seen, jnp.exp2(scaled - lse_row), 0.0))
            else:
                parts.append(jnp.exp2(scaled - jnp.where(q_fold > k_fold, lse_row, 1e30)))
        return parts

    def tile(keyed, asked, first_q, first_k, after_dv=None, after_dk=None):
        query, grad = q_buf[span(asked)], g_buf[span(asked)]
        scores = lax.dot_general(k_buf[span(keyed)], query, NT, preferred_element_type=jnp.float32)
        dprobs = lax.dot_general(v_buf[span(keyed)], grad, NT, preferred_element_type=jnp.float32)
        parts = probabilities(keyed, asked, scores)
        delta_row = stat_row(1, asked)
        lows = []
        for n in reversed(range(len(keyed))):
            j = keyed[n]
            probs = jnp.concatenate(parts[2 * n:2 * n + 2], axis=0)
            dv = jnp.dot(probs.astype(jnp.bfloat16), grad, preferred_element_type=jnp.float32)
            dv_acc[part(j)] = dv if first_k else dv_acc[part(j)] + dv
            if after_dv is not None and j == 1:
                after_dv()
            dscores = probs * (dprobs[n * rows:(n + 1) * rows] - delta_row)
            lows.insert(0, dscores.astype(jnp.bfloat16))
            dk = jnp.dot(lows[0], query, preferred_element_type=jnp.float32)
            dk_acc[part(j)] = dk if first_k else dk_acc[part(j)] + dk
            if after_dk is not None and j == 1:
                after_dk()
        low = jnp.concatenate(lows, axis=0)
        dq = lax.dot_general(low, k_buf[span(keyed)], TN, preferred_element_type=jnp.float32)
        dq_acc[span(asked)] = dq if first_q else dq_acc[span(asked)] + dq

    def send_dq(n, s, peer):
        dq_send[s - 1] = dq_acc[part(s)].astype(jnp.bfloat16)
        return send(n, dq_send.at[s - 1], dq_recv.at[s - 1], peer)

    def send_kv(n, i, acc):
        kv_send[i] = acc[part(1)].astype(jnp.bfloat16)
        return send(n, kv_send.at[i], kv_recv.at[i], to_y)

    tile([0], [0], True, True)
    q_c.wait_recv()
    g_c.wait_recv()
    st_c.wait_recv()
    tile([0], [1], True, False)
    q_x.wait_recv()
    q_r = send(9, q_buf.at[part(2)], q_buf.at[part(3)], to_core)
    g_x.wait_recv()
    g_r = send(10, g_buf.at[part(2)], g_buf.at[part(3)], to_core)
    k_y.wait_recv()
    v_y.wait_recv()
    tile([1], [0, 1], False, True)
    dq_1 = send_dq(11, 1, to_core)
    st_x.wait_recv()
    tile([0, 1], [2], True, False)
    dq_2 = send_dq(12, 2, to_x)
    q_r.wait_recv()
    g_r.wait_recv()
    st_b.wait_recv()
    late = []
    tile([0, 1], [3], True, False, lambda: late.append(send_kv(13, 0, dv_acc)),
         lambda: late.append(send_kv(14, 1, dk_acc)))
    dq_3 = send_dq(15, 3, to_both)
    dq_1.wait_recv()
    dq_2.wait_recv()
    dq_mine = (dq_acc[part(0)] + dq_recv[0].astype(jnp.float32)) + dq_recv[1].astype(jnp.float32)
    late[0].wait_recv()
    dv_out[...] = (dv_acc[part(0)] + kv_recv[0].astype(jnp.float32)).astype(jnp.bfloat16)
    late[1].wait_recv()
    dk_out[...] = (
        (dk_acc[part(0)] + kv_recv[1].astype(jnp.float32)) * factor).astype(jnp.bfloat16)
    dq_3.wait_recv()
    dq_out[...] = ((dq_mine + dq_recv[2].astype(jnp.float32)) * factor).astype(jnp.bfloat16)
    for copy in sends:
        copy.wait_send()


def store_kernel(dq_in, dk_in, dv_in, dq_out, dk_out, dv_out, sems):
    copies = []
    for n, (src, dst) in enumerate(((dq_in, dq_out), (dk_in, dk_out), (dv_in, dv_out))):
        copy = pltpu.make_async_copy(src, dst, sems.at[n])
        copy.start()
        copies.append(copy)
    for copy in copies:
        copy.wait()


def plane_body(queries, key_rows, value_rows, outputs, out_grad, saved_lse, fold_map):
    rows, width = queries.shape
    factor = 1.0 / math.sqrt(width)
    low, full = jnp.bfloat16, jnp.float32
    grad = jax.ShapeDtypeStruct((rows, width), low)
    arrays = [
        pltpu.with_memory_space_constraint(a, pltpu.HBM)
        for a in (queries, key_rows, value_rows, outputs, out_grad, saved_lse.reshape(1, rows),
                  fold_map)
    ]
    grads = pl.pallas_call(
        functools.partial(plane_kernel, rows, factor),
        out_shape=(pltpu.VMEM((rows, width), low),) * 3,
        in_specs=[pl.BlockSpec(memory_space=pl.ANY)] * 7,
        out_specs=[pl.BlockSpec(memory_space=pltpu.VMEM)] * 3,
        scratch_shapes=[
            pltpu.VMEM((4 * rows, width), low),
            pltpu.VMEM((4 * rows, width), low),
            pltpu.VMEM((2 * rows, width), low),
            pltpu.VMEM((2 * rows, width), low),
            pltpu.VMEM((rows, width), low),
            pltpu.VMEM((1, rows), low),
            pltpu.SMEM(fold_map.shape, jnp.int32),
            pltpu.VMEM((4, 8, rows), full),
            pltpu.VMEM((4 * rows, width), full),
            pltpu.VMEM((2 * rows, width), full),
            pltpu.VMEM((2 * rows, width), full),
            pltpu.VMEM((2, rows, width), low),
            pltpu.VMEM((2, rows, width), low),
            pltpu.VMEM((3, rows, width), low),
            pltpu.VMEM((3, rows, width), low),
            pltpu.SemaphoreType.DMA((7,)),
            pltpu.SemaphoreType.DMA((16,)),
            pltpu.SemaphoreType.DMA((16,)),
        ],
        compiler_params=pltpu.CompilerParams(
            collective_id=0, has_side_effects=True, vmem_limit_bytes=32 * 2**20
        ),
        cost_estimate=pl.CostEstimate(
            flops=80 * rows * rows * width,
            bytes_accessed=16 * rows * width,
            transcendentals=8 * rows * rows,
        ),
    )(*arrays)
    return pl.pallas_call(
        store_kernel,
        out_shape=(grad, grad, grad),
        in_specs=[pl.BlockSpec(memory_space=pl.ANY)] * 3,
        out_specs=[pl.BlockSpec(memory_space=pl.ANY)] * 3,
        scratch_shapes=[pltpu.SemaphoreType.DMA((3,))],
        compiler_params=pltpu.CompilerParams(vmem_limit_bytes=2**20),
    )(*[pltpu.with_memory_space_constraint(a, pltpu.VMEM) for a in grads])


def solution(mesh):
    plane = mesh.shape["pb"] == 4 and mesh.shape["ka"] == 2
    return jax.shard_map(
        plane_body if plane else body,
        mesh=mesh,
        in_specs=(
            P(("pb", "ka"), "ha"),
            P(("pb", "ka"), "ha"),
            P(("pb", "ka"), "ha"),
            P(("pb", "ka"), "ha"),
            P(("pb", "ka"), "ha"),
            P(("pb", "ka"), "ha"),
            P(),
        ),
        out_specs=(P(("pb", "ka"), "ha"), P(("pb", "ka"), "ha"), P(("pb", "ka"), "ha")),
        check_vma=False,
    )
```

```python
import functools
import math

import jax
import jax.numpy as jnp
from jax import lax
from jax.experimental import pallas as pl
from jax.experimental.pallas import tpu as pltpu
from jax.sharding import PartitionSpec as P


def block_length(row_total):
    length = row_total
    while length > 512 and length % 2 == 0:
        length = length // 2
    return length


def tile_grads(
    query_blk, grad_blk, lse_blk, delta_blk, query_pos, key_blk, value_blk, key_pos, factor
):
    scores = (
        jnp.einsum("qhd,khd->hqk", query_blk, key_blk, preferred_element_type=jnp.float32) * factor
    )
    visible = key_pos[None, :] <= query_pos[:, None]
    probs = jnp.where(visible[None], jnp.exp(scores - lse_blk.T[:, :, None]), 0.0)
    probs_low = probs.astype(jnp.bfloat16)
    value_part = jnp.einsum("hqk,qhd->khd", probs_low, grad_blk, preferred_element_type=jnp.float32)
    dprobs = jnp.einsum("qhd,khd->hqk", grad_blk, value_blk, preferred_element_type=jnp.float32)
    dscores = (probs * (dprobs - delta_blk.T[:, :, None])).astype(jnp.bfloat16)
    query_part = jnp.einsum("hqk,khd->qhd", dscores, key_blk, preferred_element_type=jnp.float32)
    key_part = jnp.einsum("hqk,qhd->khd", dscores, query_blk, preferred_element_type=jnp.float32)
    return (query_part, key_part, value_part)


def add_rows(target, update, first_row):
    length = update.shape[0]
    current = lax.dynamic_slice_in_dim(target, first_row, length, 0)
    return lax.dynamic_update_slice_in_dim(target, current + update, first_row, 0)


def body(queries, key_rows, value_rows, outputs, out_grad, saved_lse, fold_map):
    row_count, full_width = queries.shape
    head_count = saved_lse.shape[1]
    head_dim = full_width // head_count
    factor = 1.0 / math.sqrt(head_dim)
    fold_rows = row_count // 2
    size_pb = lax.axis_size("pb")
    size_ka = lax.axis_size("ka")
    index_pb = lax.axis_index("pb")
    index_ka = lax.axis_index("ka")
    key_all, value_all = (
        lax.all_gather(key_rows, "pb", axis=0, tiled=True),
        lax.all_gather(value_rows, "pb", axis=0, tiled=True),
    )
    key_len = size_pb * row_count
    key_all = key_all.reshape(key_len, head_count, head_dim)
    value_all = value_all.reshape(key_len, head_count, head_dim)
    key_iota = jnp.arange(key_len, dtype=jnp.int32)
    key_global = (key_iota // row_count * size_ka + index_ka) * row_count + key_iota % row_count
    key_pos = fold_map[key_global // fold_rows] * fold_rows + key_global % fold_rows
    query_len = size_ka * row_count
    query_first = index_pb * query_len
    query_empty = jnp.zeros((query_len, head_count, head_dim), jnp.float32)
    key_empty = jnp.zeros((key_len, head_count, head_dim), jnp.float32)
    init = (query_empty, key_empty, key_empty)
    query_src = lax.all_gather(queries, "ka", axis=0, tiled=True)
    grad_src = lax.all_gather(out_grad, "ka", axis=0, tiled=True)
    saved_src = lax.all_gather(outputs, "ka", axis=0, tiled=True)
    lse_src = lax.all_gather(saved_lse, "ka", axis=0, tiled=True)
    piece_rows = query_src.shape[0]
    step_rows = block_length(piece_rows)

    def one_block(number, state):
        dq_all, dk_all, dv_all = state
        offset = number * step_rows
        query_blk = lax.dynamic_slice_in_dim(query_src, offset, step_rows, 0).reshape(
            step_rows, head_count, head_dim
        )
        grad_blk = lax.dynamic_slice_in_dim(grad_src, offset, step_rows, 0).reshape(
            step_rows, head_count, head_dim
        )
        lse_blk = lax.dynamic_slice_in_dim(lse_src, offset, step_rows, 0).astype(jnp.float32)
        saved_blk = lax.dynamic_slice_in_dim(saved_src, offset, step_rows, 0).reshape(
            step_rows, head_count, head_dim
        )
        delta_low = jnp.einsum(
            "qhd,qhd->qh", grad_blk, saved_blk, preferred_element_type=jnp.float32
        ).astype(jnp.bfloat16)
        delta_blk = lax.optimization_barrier(delta_low).astype(jnp.float32)
        row_global = query_first + offset + jnp.arange(step_rows, dtype=jnp.int32)
        query_pos = fold_map[row_global // fold_rows] * fold_rows + row_global % fold_rows
        dq_blk, dk_part, dv_part = tile_grads(
            query_blk, grad_blk, lse_blk, delta_blk, query_pos, key_all, value_all, key_pos, factor
        )
        dk_all = dk_all + dk_part
        dv_all = dv_all + dv_part
        dq_all = add_rows(dq_all, dq_blk, offset)
        return (dq_all, dk_all, dv_all)

    dq_all, dk_all, dv_all = lax.fori_loop(0, piece_rows // step_rows, one_block, init)
    query_mine = lax.psum_scatter(
        dq_all.reshape(query_len, full_width), "ka", scatter_dimension=0, tiled=True
    )
    query_grad = (query_mine * factor).astype(jnp.bfloat16)
    key_flat = dk_all.reshape(key_len, full_width)
    value_flat = dv_all.reshape(key_len, full_width)
    key_total, value_total = lax.psum((key_flat, value_flat), "pb")
    key_mine = lax.dynamic_slice_in_dim(key_total, index_pb * row_count, row_count, 0)
    value_mine = lax.dynamic_slice_in_dim(value_total, index_pb * row_count, row_count, 0)
    key_grad = (key_mine * factor).astype(jnp.bfloat16)
    value_grad = value_mine.astype(jnp.bfloat16)
    return (query_grad, key_grad, value_grad)


MESH = pl.DeviceIdType.MESH
NT = (((1,), (1,)), ((), ()))
TN = (((0,), (0,)), ((), ()))


def plane_kernel(
    rows, factor,
    q_in, k_in, v_in, o_in, g_in, lse_in, map_in,
    dq_out, dk_out, dv_out,
    q_buf, g_buf, k_buf, v_buf, o_buf, lse_buf, map_buf, stat,
    dq_acc, dk_acc, dv_acc,
    kv_send, kv_recv, dq_send, dq_recv,
    local_sem, send_sem, recv_sem,
):
    p = lax.axis_index("pb")
    x = lax.axis_index("ka")
    h = lax.axis_index("ha")
    c = lax.rem(p, 2)
    y = p // 2
    p_core = p + 1 - 2 * c
    p_far = lax.rem(p + 2, 4)
    to_core = (p_core, x, h)
    to_x = (p, 1 - x, h)
    to_y = (p_far, x, h)
    to_both = (p_core, 1 - x, h)
    fold_rows = rows // 2

    def part(slot):
        return pl.ds(slot * rows, rows)

    barrier = pltpu.get_barrier_semaphore()
    for peer in (to_core, to_x, to_y, to_both):
        pl.semaphore_signal(barrier, inc=1, device_id=peer, device_id_type=MESH)
    locals_ = []
    for n, (src, dst) in enumerate((
        (g_in, g_buf.at[part(0)]), (o_in, o_buf), (lse_in, lse_buf), (q_in, q_buf.at[part(0)]),
        (k_in, k_buf.at[part(0)]), (v_in, v_buf.at[part(0)]), (map_in, map_buf),
    )):
        copy = pltpu.make_async_copy(src, dst, local_sem.at[n])
        copy.start()
        locals_.append(copy)
    pl.semaphore_wait(barrier, 4)

    sends = []

    def send(n, src, dst, peer):
        copy = pltpu.make_async_remote_copy(
            src_ref=src, dst_ref=dst, send_sem=send_sem.at[n], recv_sem=recv_sem.at[n],
            device_id=peer, device_id_type=MESH,
        )
        copy.start()
        sends.append(copy)
        return copy

    q_x = send(0, q_in, q_buf.at[part(2)], to_x)
    k_y = send(1, k_in, k_buf.at[part(1)], to_y)
    q_c = send(2, q_in, q_buf.at[part(1)], to_core)
    g_c = send(3, g_in, g_buf.at[part(1)], to_core)
    g_x = send(4, g_in, g_buf.at[part(2)], to_x)
    v_y = send(5, v_in, v_buf.at[part(1)], to_y)

    for copy in locals_[:3]:
        copy.wait()
    gram = lax.dot_general(o_buf[...], g_buf[part(0)], NT, preferred_element_type=jnp.float32)
    down = lax.broadcasted_iota(jnp.int32, (rows, rows), 0)
    along = lax.broadcasted_iota(jnp.int32, (rows, rows), 1)
    delta = jnp.sum(jnp.where(down == along, gram, 0.0), axis=0, keepdims=True)
    delta = delta.astype(jnp.bfloat16).astype(jnp.float32)
    log2e = math.log2(math.e)
    lse = lse_buf[...].astype(jnp.float32) * log2e
    which = lax.broadcasted_iota(jnp.int32, (8, rows), 0)
    stat[0] = jnp.where(which == 0, lse, delta)
    st_c = send(6, stat.at[0], stat.at[1], to_core)
    st_x = send(7, stat.at[0], stat.at[2], to_x)
    st_b = send(8, stat.at[0], stat.at[3], to_both)
    for copy in locals_[3:]:
        copy.wait()

    q_owner = (p * 2 + x, p_core * 2 + x, p * 2 + 1 - x, p_core * 2 + 1 - x)
    k_owner = (p * 2 + x, p_far * 2 + x)
    half = lax.broadcasted_iota(jnp.int32, (1, rows), 1) // fold_rows
    lane = lax.broadcasted_iota(jnp.int32, (fold_rows, rows), 1) % fold_rows
    level = lax.broadcasted_iota(jnp.int32, (fold_rows, rows), 0)

    def span(slots):
        return pl.ds(slots[0] * rows, len(slots) * rows)

    def stat_row(n, slots):
        return jnp.concatenate([stat[s, n:n + 1, :] for s in slots], axis=1)

    def probabilities(keyed, asked, scores):
        own = keyed == [0] and asked == [0]
        q_fold = jnp.concatenate([
            jnp.where(half == 0, map_buf[q_owner[s] * 2], map_buf[q_owner[s] * 2 + 1])
            for s in asked], axis=1)
        lse_row = stat_row(0, asked)
        parts = []
        for n in range(2 * len(keyed)):
            k_fold = map_buf[k_owner[keyed[n // 2]] * 2 + n % 2]
            scaled = scores[n * fold_rows:(n + 1) * fold_rows] * (factor * log2e)
            if own:
                seen = k_fold * fold_rows + level <= q_fold * fold_rows + lane
                parts.append(jnp.where(seen, jnp.exp2(scaled - lse_row), 0.0))
            else:
                parts.append(jnp.exp2(scaled - jnp.where(q_fold > k_fold, lse_row, 1e30)))
        return parts

    def score_stage(keyed, asked):
        scores = lax.dot_general(
            k_buf[span(keyed)], q_buf[span(asked)], NT, preferred_element_type=jnp.float32)
        return probabilities(keyed, asked, scores)

    def grad_stage(keyed, asked, parts, first_q, first_k, after_dv=None, after_dk=None):
        query, grad = q_buf[span(asked)], g_buf[span(asked)]
        dprobs = lax.dot_general(v_buf[span(keyed)], grad, NT, preferred_element_type=jnp.float32)
        delta_row = stat_row(1, asked)
        lows = []
        for n in reversed(range(len(keyed))):
            j = keyed[n]
            probs = jnp.concatenate(parts[2 * n:2 * n + 2], axis=0)
            dv = jnp.dot(probs.astype(jnp.bfloat16), grad, preferred_element_type=jnp.float32)
            dv_acc[part(j)] = dv if first_k else dv_acc[part(j)] + dv
            if after_dv is not None and j == 1:
                after_dv()
            dscores = probs * (dprobs[n * rows:(n + 1) * rows] - delta_row)
            lows.insert(0, dscores.astype(jnp.bfloat16))
            dk = jnp.dot(lows[0], query, preferred_element_type=jnp.float32)
            dk_acc[part(j)] = dk if first_k else dk_acc[part(j)] + dk
            if after_dk is not None and j == 1:
                after_dk()
        low = jnp.concatenate(lows, axis=0)
        dq = lax.dot_general(low, k_buf[span(keyed)], TN, preferred_element_type=jnp.float32)
        dq_acc[span(asked)] = dq if first_q else dq_acc[span(asked)] + dq

    def send_dq(n, s, peer):
        dq_send[s - 1] = dq_acc[part(s)].astype(jnp.bfloat16)
        return send(n, dq_send.at[s - 1], dq_recv.at[s - 1], peer)

    def send_kv(n, i, acc):
        kv_send[i] = acc[part(1)].astype(jnp.bfloat16)
        return send(n, kv_send.at[i], kv_recv.at[i], to_y)

    grad_stage([0], [0], score_stage([0], [0]), True, True)
    q_c.wait_recv()
    g_c.wait_recv()
    st_c.wait_recv()
    grad_stage([0], [1], score_stage([0], [1]), True, False)
    q_x.wait_recv()
    q_r = send(9, q_buf.at[part(2)], q_buf.at[part(3)], to_core)
    k_y.wait_recv()
    near = score_stage([1], [0, 1])
    st_x.wait_recv()
    across = score_stage([0, 1], [2])
    q_r.wait_recv()
    st_b.wait_recv()
    corner = score_stage([0, 1], [3])
    g_x.wait_recv()
    g_r = send(10, g_buf.at[part(2)], g_buf.at[part(3)], to_core)
    v_y.wait_recv()
    grad_stage([1], [0, 1], near, False, True)
    dq_1 = send_dq(11, 1, to_core)
    grad_stage([0, 1], [2], across, True, False)
    dq_2 = send_dq(12, 2, to_x)
    g_r.wait_recv()
    late = []
    grad_stage([0, 1], [3], corner, True, False, lambda: late.append(send_kv(13, 0, dv_acc)),
               lambda: late.append(send_kv(14, 1, dk_acc)))
    dq_3 = send_dq(15, 3, to_both)
    dq_1.wait_recv()
    dq_2.wait_recv()
    dq_mine = (dq_acc[part(0)] + dq_recv[0].astype(jnp.float32)) + dq_recv[1].astype(jnp.float32)
    late[0].wait_recv()
    dv_out[...] = (dv_acc[part(0)] + kv_recv[0].astype(jnp.float32)).astype(jnp.bfloat16)
    late[1].wait_recv()
    dk_out[...] = (
        (dk_acc[part(0)] + kv_recv[1].astype(jnp.float32)) * factor).astype(jnp.bfloat16)
    dq_3.wait_recv()
    dq_out[...] = ((dq_mine + dq_recv[2].astype(jnp.float32)) * factor).astype(jnp.bfloat16)
    for copy in sends:
        copy.wait_send()


def store_kernel(dq_in, dk_in, dv_in, dq_out, dk_out, dv_out, sems):
    copies = []
    for n, (src, dst) in enumerate(((dq_in, dq_out), (dk_in, dk_out), (dv_in, dv_out))):
        copy = pltpu.make_async_copy(src, dst, sems.at[n])
        copy.start()
        copies.append(copy)
    for copy in copies:
        copy.wait()


def plane_body(queries, key_rows, value_rows, outputs, out_grad, saved_lse, fold_map):
    rows, width = queries.shape
    factor = 1.0 / math.sqrt(width)
    low, full = jnp.bfloat16, jnp.float32
    grad = jax.ShapeDtypeStruct((rows, width), low)
    arrays = [
        pltpu.with_memory_space_constraint(a, pltpu.HBM)
        for a in (queries, key_rows, value_rows, outputs, out_grad, saved_lse.reshape(1, rows),
                  fold_map)
    ]
    grads = pl.pallas_call(
        functools.partial(plane_kernel, rows, factor),
        out_shape=(pltpu.VMEM((rows, width), low),) * 3,
        in_specs=[pl.BlockSpec(memory_space=pl.ANY)] * 7,
        out_specs=[pl.BlockSpec(memory_space=pltpu.VMEM)] * 3,
        scratch_shapes=[
            pltpu.VMEM((4 * rows, width), low),
            pltpu.VMEM((4 * rows, width), low),
            pltpu.VMEM((2 * rows, width), low),
            pltpu.VMEM((2 * rows, width), low),
            pltpu.VMEM((rows, width), low),
            pltpu.VMEM((1, rows), low),
            pltpu.SMEM(fold_map.shape, jnp.int32),
            pltpu.VMEM((4, 8, rows), full),
            pltpu.VMEM((4 * rows, width), full),
            pltpu.VMEM((2 * rows, width), full),
            pltpu.VMEM((2 * rows, width), full),
            pltpu.VMEM((2, rows, width), low),
            pltpu.VMEM((2, rows, width), low),
            pltpu.VMEM((3, rows, width), low),
            pltpu.VMEM((3, rows, width), low),
            pltpu.SemaphoreType.DMA((7,)),
            pltpu.SemaphoreType.DMA((16,)),
            pltpu.SemaphoreType.DMA((16,)),
        ],
        compiler_params=pltpu.CompilerParams(
            collective_id=0, has_side_effects=True, vmem_limit_bytes=32 * 2**20
        ),
        cost_estimate=pl.CostEstimate(
            flops=80 * rows * rows * width,
            bytes_accessed=16 * rows * width,
            transcendentals=8 * rows * rows,
        ),
    )(*arrays)
    return pl.pallas_call(
        store_kernel,
        out_shape=(grad, grad, grad),
        in_specs=[pl.BlockSpec(memory_space=pl.ANY)] * 3,
        out_specs=[pl.BlockSpec(memory_space=pl.ANY)] * 3,
        scratch_shapes=[pltpu.SemaphoreType.DMA((3,))],
        compiler_params=pltpu.CompilerParams(vmem_limit_bytes=2**20),
    )(*[pltpu.with_memory_space_constraint(a, pltpu.VMEM) for a in grads])


def solution(mesh):
    plane = mesh.shape["pb"] == 4 and mesh.shape["ka"] == 2
    return jax.shard_map(
        plane_body if plane else body,
        mesh=mesh,
        in_specs=(
            P(("pb", "ka"), "ha"),
            P(("pb", "ka"), "ha"),
            P(("pb", "ka"), "ha"),
            P(("pb", "ka"), "ha"),
            P(("pb", "ka"), "ha"),
            P(("pb", "ka"), "ha"),
            P(),
        ),
        out_specs=(P(("pb", "ka"), "ha"), P(("pb", "ka"), "ha"), P(("pb", "ka"), "ha")),
        check_vma=False,
    )
```

```python
import functools
import math

import jax
import jax.numpy as jnp
from jax import lax
from jax.experimental import pallas as pl
from jax.experimental.pallas import tpu as pltpu
from jax.sharding import PartitionSpec as P


def block_length(row_total):
    length = row_total
    while length > 512 and length % 2 == 0:
        length = length // 2
    return length


def tile_grads(
    query_blk, grad_blk, lse_blk, delta_blk, query_pos, key_blk, value_blk, key_pos, factor
):
    scores = (
        jnp.einsum("qhd,khd->hqk", query_blk, key_blk, preferred_element_type=jnp.float32) * factor
    )
    visible = key_pos[None, :] <= query_pos[:, None]
    probs = jnp.where(visible[None], jnp.exp(scores - lse_blk.T[:, :, None]), 0.0)
    probs_low = probs.astype(jnp.bfloat16)
    value_part = jnp.einsum("hqk,qhd->khd", probs_low, grad_blk, preferred_element_type=jnp.float32)
    dprobs = jnp.einsum("qhd,khd->hqk", grad_blk, value_blk, preferred_element_type=jnp.float32)
    dscores = (probs * (dprobs - delta_blk.T[:, :, None])).astype(jnp.bfloat16)
    query_part = jnp.einsum("hqk,khd->qhd", dscores, key_blk, preferred_element_type=jnp.float32)
    key_part = jnp.einsum("hqk,qhd->khd", dscores, query_blk, preferred_element_type=jnp.float32)
    return (query_part, key_part, value_part)


def add_rows(target, update, first_row):
    length = update.shape[0]
    current = lax.dynamic_slice_in_dim(target, first_row, length, 0)
    return lax.dynamic_update_slice_in_dim(target, current + update, first_row, 0)


def body(queries, key_rows, value_rows, outputs, out_grad, saved_lse, fold_map):
    row_count, full_width = queries.shape
    head_count = saved_lse.shape[1]
    head_dim = full_width // head_count
    factor = 1.0 / math.sqrt(head_dim)
    fold_rows = row_count // 2
    size_pb = lax.axis_size("pb")
    size_ka = lax.axis_size("ka")
    index_pb = lax.axis_index("pb")
    index_ka = lax.axis_index("ka")
    key_all, value_all = (
        lax.all_gather(key_rows, "pb", axis=0, tiled=True),
        lax.all_gather(value_rows, "pb", axis=0, tiled=True),
    )
    key_len = size_pb * row_count
    key_all = key_all.reshape(key_len, head_count, head_dim)
    value_all = value_all.reshape(key_len, head_count, head_dim)
    key_iota = jnp.arange(key_len, dtype=jnp.int32)
    key_global = (key_iota // row_count * size_ka + index_ka) * row_count + key_iota % row_count
    key_pos = fold_map[key_global // fold_rows] * fold_rows + key_global % fold_rows
    query_len = size_ka * row_count
    query_first = index_pb * query_len
    query_empty = jnp.zeros((query_len, head_count, head_dim), jnp.float32)
    key_empty = jnp.zeros((key_len, head_count, head_dim), jnp.float32)
    init = (query_empty, key_empty, key_empty)
    query_src = lax.all_gather(queries, "ka", axis=0, tiled=True)
    grad_src = lax.all_gather(out_grad, "ka", axis=0, tiled=True)
    saved_src = lax.all_gather(outputs, "ka", axis=0, tiled=True)
    lse_src = lax.all_gather(saved_lse, "ka", axis=0, tiled=True)
    piece_rows = query_src.shape[0]
    step_rows = block_length(piece_rows)

    def one_block(number, state):
        dq_all, dk_all, dv_all = state
        offset = number * step_rows
        query_blk = lax.dynamic_slice_in_dim(query_src, offset, step_rows, 0).reshape(
            step_rows, head_count, head_dim
        )
        grad_blk = lax.dynamic_slice_in_dim(grad_src, offset, step_rows, 0).reshape(
            step_rows, head_count, head_dim
        )
        lse_blk = lax.dynamic_slice_in_dim(lse_src, offset, step_rows, 0).astype(jnp.float32)
        saved_blk = lax.dynamic_slice_in_dim(saved_src, offset, step_rows, 0).reshape(
            step_rows, head_count, head_dim
        )
        delta_low = jnp.einsum(
            "qhd,qhd->qh", grad_blk, saved_blk, preferred_element_type=jnp.float32
        ).astype(jnp.bfloat16)
        delta_blk = lax.optimization_barrier(delta_low).astype(jnp.float32)
        row_global = query_first + offset + jnp.arange(step_rows, dtype=jnp.int32)
        query_pos = fold_map[row_global // fold_rows] * fold_rows + row_global % fold_rows
        dq_blk, dk_part, dv_part = tile_grads(
            query_blk, grad_blk, lse_blk, delta_blk, query_pos, key_all, value_all, key_pos, factor
        )
        dk_all = dk_all + dk_part
        dv_all = dv_all + dv_part
        dq_all = add_rows(dq_all, dq_blk, offset)
        return (dq_all, dk_all, dv_all)

    dq_all, dk_all, dv_all = lax.fori_loop(0, piece_rows // step_rows, one_block, init)
    query_mine = lax.psum_scatter(
        dq_all.reshape(query_len, full_width), "ka", scatter_dimension=0, tiled=True
    )
    query_grad = (query_mine * factor).astype(jnp.bfloat16)
    key_flat = dk_all.reshape(key_len, full_width)
    value_flat = dv_all.reshape(key_len, full_width)
    key_total, value_total = lax.psum((key_flat, value_flat), "pb")
    key_mine = lax.dynamic_slice_in_dim(key_total, index_pb * row_count, row_count, 0)
    value_mine = lax.dynamic_slice_in_dim(value_total, index_pb * row_count, row_count, 0)
    key_grad = (key_mine * factor).astype(jnp.bfloat16)
    value_grad = value_mine.astype(jnp.bfloat16)
    return (query_grad, key_grad, value_grad)


MESH = pl.DeviceIdType.MESH
NT = (((1,), (1,)), ((), ()))
TN = (((0,), (0,)), ((), ()))


def plane_kernel(
    rows, factor,
    q_in, k_in, v_in, o_in, g_in, lse_in, map_in,
    dq_out, dk_out, dv_out,
    q_buf, g_buf, k_buf, v_buf, o_buf, lse_buf, map_buf, stat,
    dq_acc, dk_acc, dv_acc,
    kv_send, kv_recv, dq_send, dq_recv,
    local_sem, send_sem, recv_sem,
):
    p = lax.axis_index("pb")
    x = lax.axis_index("ka")
    h = lax.axis_index("ha")
    c = lax.rem(p, 2)
    y = p // 2
    p_core = p + 1 - 2 * c
    p_far = lax.rem(p + 2, 4)
    to_core = (p_core, x, h)
    to_x = (p, 1 - x, h)
    to_y = (p_far, x, h)
    to_both = (p_core, 1 - x, h)
    fold_rows = rows // 2

    def part(slot):
        return pl.ds(slot * rows, rows)

    barrier = pltpu.get_barrier_semaphore()
    for peer in (to_core, to_x, to_y, to_both):
        pl.semaphore_signal(barrier, inc=1, device_id=peer, device_id_type=MESH)
    locals_ = []
    for n, (src, dst) in enumerate((
        (g_in, g_buf.at[part(0)]), (o_in, o_buf), (lse_in, lse_buf), (q_in, q_buf.at[part(0)]),
        (k_in, k_buf.at[part(0)]), (v_in, v_buf.at[part(0)]), (map_in, map_buf),
    )):
        copy = pltpu.make_async_copy(src, dst, local_sem.at[n])
        copy.start()
        locals_.append(copy)
    pl.semaphore_wait(barrier, 4)

    sends = []

    def send(n, src, dst, peer):
        copy = pltpu.make_async_remote_copy(
            src_ref=src, dst_ref=dst, send_sem=send_sem.at[n], recv_sem=recv_sem.at[n],
            device_id=peer, device_id_type=MESH,
        )
        copy.start()
        sends.append(copy)
        return copy

    q_x = send(0, q_in, q_buf.at[part(2)], to_x)
    k_y = send(1, k_in, k_buf.at[part(1)], to_y)
    q_c = send(2, q_in, q_buf.at[part(1)], to_core)
    g_c = send(3, g_in, g_buf.at[part(1)], to_core)
    g_x = send(4, g_in, g_buf.at[part(2)], to_x)
    v_y = send(5, v_in, v_buf.at[part(1)], to_y)

    for copy in locals_[:3]:
        copy.wait()
    gram = lax.dot_general(o_buf[...], g_buf[part(0)], NT, preferred_element_type=jnp.float32)
    down = lax.broadcasted_iota(jnp.int32, (rows, rows), 0)
    along = lax.broadcasted_iota(jnp.int32, (rows, rows), 1)
    delta = jnp.sum(jnp.where(down == along, gram, 0.0), axis=0, keepdims=True)
    delta = delta.astype(jnp.bfloat16).astype(jnp.float32)
    log2e = math.log2(math.e)
    lse = lse_buf[...].astype(jnp.float32) * log2e
    which = lax.broadcasted_iota(jnp.int32, (8, rows), 0)
    stat[0] = jnp.where(which == 0, lse, delta)
    st_c = send(6, stat.at[0], stat.at[1], to_core)
    st_x = send(7, stat.at[0], stat.at[2], to_x)
    st_b = send(8, stat.at[0], stat.at[3], to_both)
    for copy in locals_[3:]:
        copy.wait()

    q_owner = (p * 2 + x, p_core * 2 + x, p * 2 + 1 - x, p_core * 2 + 1 - x)
    k_owner = (p * 2 + x, p_far * 2 + x)
    half = lax.broadcasted_iota(jnp.int32, (1, rows), 1) // fold_rows
    lane = lax.broadcasted_iota(jnp.int32, (fold_rows, rows), 1) % fold_rows
    level = lax.broadcasted_iota(jnp.int32, (fold_rows, rows), 0)

    def span(slots):
        return pl.ds(slots[0] * rows, len(slots) * rows)

    def stat_row(n, slots):
        return jnp.concatenate([stat[s, n:n + 1, :] for s in slots], axis=1)

    def probabilities(keyed, asked, scores):
        own = keyed == [0] and asked == [0]
        q_fold = jnp.concatenate([
            jnp.where(half == 0, map_buf[q_owner[s] * 2], map_buf[q_owner[s] * 2 + 1])
            for s in asked], axis=1)
        lse_row = stat_row(0, asked)
        parts = []
        for n in range(2 * len(keyed)):
            k_fold = map_buf[k_owner[keyed[n // 2]] * 2 + n % 2]
            scaled = scores[n * fold_rows:(n + 1) * fold_rows] * (factor * log2e)
            if own:
                seen = k_fold * fold_rows + level <= q_fold * fold_rows + lane
                parts.append(jnp.where(seen, jnp.exp2(scaled - lse_row), 0.0))
            else:
                parts.append(jnp.exp2(scaled - jnp.where(q_fold > k_fold, lse_row, 1e30)))
        return parts

    def tile(keyed, asked, first_q, first_k, after_dv=None, after_dk=None):
        query, grad = q_buf[span(asked)], g_buf[span(asked)]
        scores = lax.dot_general(k_buf[span(keyed)], query, NT, preferred_element_type=jnp.float32)
        dprobs = lax.dot_general(v_buf[span(keyed)], grad, NT, preferred_element_type=jnp.float32)
        parts = probabilities(keyed, asked, scores)
        delta_row = stat_row(1, asked)
        lows = []
        for n in reversed(range(len(keyed))):
            j = keyed[n]
            probs = jnp.concatenate(parts[2 * n:2 * n + 2], axis=0)
            dv = jnp.dot(probs.astype(jnp.bfloat16), grad, preferred_element_type=jnp.float32)
            dv_acc[part(j)] = dv if first_k else dv_acc[part(j)] + dv
            if after_dv is not None and j == 1:
                after_dv()
            dscores = probs * (dprobs[n * rows:(n + 1) * rows] - delta_row)
            lows.insert(0, dscores.astype(jnp.bfloat16))
            dk = jnp.dot(lows[0], query, preferred_element_type=jnp.float32)
            dk_acc[part(j)] = dk if first_k else dk_acc[part(j)] + dk
            if after_dk is not None and j == 1:
                after_dk()
        low = jnp.concatenate(lows, axis=0)
        dq = lax.dot_general(k_buf[span(keyed)], low, TN, preferred_element_type=jnp.float32)
        dq_acc[:, span(asked)] = dq if first_q else dq_acc[:, span(asked)] + dq

    def send_dq(n, s, peer):
        dq_send[s - 1] = dq_acc[:, part(s)].astype(jnp.bfloat16)
        return send(n, dq_send.at[s - 1], dq_recv.at[s - 1], peer)

    def send_kv(n, i, acc):
        kv_send[i] = acc[part(1)].astype(jnp.bfloat16)
        return send(n, kv_send.at[i], kv_recv.at[i], to_y)

    tile([0], [0], True, True)
    q_c.wait_recv()
    g_c.wait_recv()
    st_c.wait_recv()
    tile([0], [1], True, False)
    q_x.wait_recv()
    q_r = send(9, q_buf.at[part(2)], q_buf.at[part(3)], to_core)
    g_x.wait_recv()
    g_r = send(10, g_buf.at[part(2)], g_buf.at[part(3)], to_core)
    k_y.wait_recv()
    v_y.wait_recv()
    tile([1], [0, 1], False, True)
    dq_1 = send_dq(11, 1, to_core)
    st_x.wait_recv()
    tile([0, 1], [2], True, False)
    dq_2 = send_dq(12, 2, to_x)
    q_r.wait_recv()
    g_r.wait_recv()
    st_b.wait_recv()
    late = []
    tile([0, 1], [3], True, False, lambda: late.append(send_kv(13, 0, dv_acc)),
         lambda: late.append(send_kv(14, 1, dk_acc)))
    dq_3 = send_dq(15, 3, to_both)
    dq_1.wait_recv()
    dq_2.wait_recv()
    dq_mine = (dq_acc[:, part(0)] + dq_recv[0].astype(jnp.float32)) + dq_recv[1].astype(jnp.float32)
    late[0].wait_recv()
    dv_out[...] = (dv_acc[part(0)] + kv_recv[0].astype(jnp.float32)).astype(jnp.bfloat16)
    late[1].wait_recv()
    dk_out[...] = (
        (dk_acc[part(0)] + kv_recv[1].astype(jnp.float32)) * factor).astype(jnp.bfloat16)
    dq_3.wait_recv()
    dq_mine = ((dq_mine + dq_recv[2].astype(jnp.float32)) * factor).T
    dq_out[...] = dq_mine.astype(jnp.bfloat16)
    for copy in sends:
        copy.wait_send()


def store_kernel(dq_in, dk_in, dv_in, dq_out, dk_out, dv_out, sems):
    copies = []
    for n, (src, dst) in enumerate(((dq_in, dq_out), (dk_in, dk_out), (dv_in, dv_out))):
        copy = pltpu.make_async_copy(src, dst, sems.at[n])
        copy.start()
        copies.append(copy)
    for copy in copies:
        copy.wait()


def plane_body(queries, key_rows, value_rows, outputs, out_grad, saved_lse, fold_map):
    rows, width = queries.shape
    factor = 1.0 / math.sqrt(width)
    low, full = jnp.bfloat16, jnp.float32
    grad = jax.ShapeDtypeStruct((rows, width), low)
    arrays = [
        pltpu.with_memory_space_constraint(a, pltpu.HBM)
        for a in (queries, key_rows, value_rows, outputs, out_grad, saved_lse.reshape(1, rows),
                  fold_map)
    ]
    grads = pl.pallas_call(
        functools.partial(plane_kernel, rows, factor),
        out_shape=(pltpu.VMEM((rows, width), low),) * 3,
        in_specs=[pl.BlockSpec(memory_space=pl.ANY)] * 7,
        out_specs=[pl.BlockSpec(memory_space=pltpu.VMEM)] * 3,
        scratch_shapes=[
            pltpu.VMEM((4 * rows, width), low),
            pltpu.VMEM((4 * rows, width), low),
            pltpu.VMEM((2 * rows, width), low),
            pltpu.VMEM((2 * rows, width), low),
            pltpu.VMEM((rows, width), low),
            pltpu.VMEM((1, rows), low),
            pltpu.SMEM(fold_map.shape, jnp.int32),
            pltpu.VMEM((4, 8, rows), full),
            pltpu.VMEM((width, 4 * rows), full),
            pltpu.VMEM((2 * rows, width), full),
            pltpu.VMEM((2 * rows, width), full),
            pltpu.VMEM((2, rows, width), low),
            pltpu.VMEM((2, rows, width), low),
            pltpu.VMEM((3, width, rows), low),
            pltpu.VMEM((3, width, rows), low),
            pltpu.SemaphoreType.DMA((7,)),
            pltpu.SemaphoreType.DMA((16,)),
            pltpu.SemaphoreType.DMA((16,)),
        ],
        compiler_params=pltpu.CompilerParams(
            collective_id=0, has_side_effects=True, vmem_limit_bytes=32 * 2**20
        ),
        cost_estimate=pl.CostEstimate(
            flops=80 * rows * rows * width,
            bytes_accessed=16 * rows * width,
            transcendentals=8 * rows * rows,
        ),
    )(*arrays)
    return pl.pallas_call(
        store_kernel,
        out_shape=(grad, grad, grad),
        in_specs=[pl.BlockSpec(memory_space=pl.ANY)] * 3,
        out_specs=[pl.BlockSpec(memory_space=pl.ANY)] * 3,
        scratch_shapes=[pltpu.SemaphoreType.DMA((3,))],
        compiler_params=pltpu.CompilerParams(vmem_limit_bytes=2**20),
    )(*[pltpu.with_memory_space_constraint(a, pltpu.VMEM) for a in grads])


def solution(mesh):
    plane = mesh.shape["pb"] == 4 and mesh.shape["ka"] == 2
    return jax.shard_map(
        plane_body if plane else body,
        mesh=mesh,
        in_specs=(
            P(("pb", "ka"), "ha"),
            P(("pb", "ka"), "ha"),
            P(("pb", "ka"), "ha"),
            P(("pb", "ka"), "ha"),
            P(("pb", "ka"), "ha"),
            P(("pb", "ka"), "ha"),
            P(),
        ),
        out_specs=(P(("pb", "ka"), "ha"), P(("pb", "ka"), "ha"), P(("pb", "ka"), "ha")),
        check_vma=False,
    )
```

```python
import functools
import math

import jax
import jax.numpy as jnp
from jax import lax
from jax.experimental import pallas as pl
from jax.experimental.pallas import tpu as pltpu
from jax.sharding import PartitionSpec as P


def block_length(row_total):
    length = row_total
    while length > 512 and length % 2 == 0:
        length = length // 2
    return length


def tile_grads(
    query_blk, grad_blk, lse_blk, delta_blk, query_pos, key_blk, value_blk, key_pos, factor
):
    scores = (
        jnp.einsum("qhd,khd->hqk", query_blk, key_blk, preferred_element_type=jnp.float32) * factor
    )
    visible = key_pos[None, :] <= query_pos[:, None]
    probs = jnp.where(visible[None], jnp.exp(scores - lse_blk.T[:, :, None]), 0.0)
    probs_low = probs.astype(jnp.bfloat16)
    value_part = jnp.einsum("hqk,qhd->khd", probs_low, grad_blk, preferred_element_type=jnp.float32)
    dprobs = jnp.einsum("qhd,khd->hqk", grad_blk, value_blk, preferred_element_type=jnp.float32)
    dscores = (probs * (dprobs - delta_blk.T[:, :, None])).astype(jnp.bfloat16)
    query_part = jnp.einsum("hqk,khd->qhd", dscores, key_blk, preferred_element_type=jnp.float32)
    key_part = jnp.einsum("hqk,qhd->khd", dscores, query_blk, preferred_element_type=jnp.float32)
    return (query_part, key_part, value_part)


def add_rows(target, update, first_row):
    length = update.shape[0]
    current = lax.dynamic_slice_in_dim(target, first_row, length, 0)
    return lax.dynamic_update_slice_in_dim(target, current + update, first_row, 0)


def body(queries, key_rows, value_rows, outputs, out_grad, saved_lse, fold_map):
    row_count, full_width = queries.shape
    head_count = saved_lse.shape[1]
    head_dim = full_width // head_count
    factor = 1.0 / math.sqrt(head_dim)
    fold_rows = row_count // 2
    size_pb = lax.axis_size("pb")
    size_ka = lax.axis_size("ka")
    index_pb = lax.axis_index("pb")
    index_ka = lax.axis_index("ka")
    key_all, value_all = (
        lax.all_gather(key_rows, "pb", axis=0, tiled=True),
        lax.all_gather(value_rows, "pb", axis=0, tiled=True),
    )
    key_len = size_pb * row_count
    key_all = key_all.reshape(key_len, head_count, head_dim)
    value_all = value_all.reshape(key_len, head_count, head_dim)
    key_iota = jnp.arange(key_len, dtype=jnp.int32)
    key_global = (key_iota // row_count * size_ka + index_ka) * row_count + key_iota % row_count
    key_pos = fold_map[key_global // fold_rows] * fold_rows + key_global % fold_rows
    query_len = size_ka * row_count
    query_first = index_pb * query_len
    query_empty = jnp.zeros((query_len, head_count, head_dim), jnp.float32)
    key_empty = jnp.zeros((key_len, head_count, head_dim), jnp.float32)
    init = (query_empty, key_empty, key_empty)
    query_src = lax.all_gather(queries, "ka", axis=0, tiled=True)
    grad_src = lax.all_gather(out_grad, "ka", axis=0, tiled=True)
    saved_src = lax.all_gather(outputs, "ka", axis=0, tiled=True)
    lse_src = lax.all_gather(saved_lse, "ka", axis=0, tiled=True)
    piece_rows = query_src.shape[0]
    step_rows = block_length(piece_rows)

    def one_block(number, state):
        dq_all, dk_all, dv_all = state
        offset = number * step_rows
        query_blk = lax.dynamic_slice_in_dim(query_src, offset, step_rows, 0).reshape(
            step_rows, head_count, head_dim
        )
        grad_blk = lax.dynamic_slice_in_dim(grad_src, offset, step_rows, 0).reshape(
            step_rows, head_count, head_dim
        )
        lse_blk = lax.dynamic_slice_in_dim(lse_src, offset, step_rows, 0).astype(jnp.float32)
        saved_blk = lax.dynamic_slice_in_dim(saved_src, offset, step_rows, 0).reshape(
            step_rows, head_count, head_dim
        )
        delta_low = jnp.einsum(
            "qhd,qhd->qh", grad_blk, saved_blk, preferred_element_type=jnp.float32
        ).astype(jnp.bfloat16)
        delta_blk = lax.optimization_barrier(delta_low).astype(jnp.float32)
        row_global = query_first + offset + jnp.arange(step_rows, dtype=jnp.int32)
        query_pos = fold_map[row_global // fold_rows] * fold_rows + row_global % fold_rows
        dq_blk, dk_part, dv_part = tile_grads(
            query_blk, grad_blk, lse_blk, delta_blk, query_pos, key_all, value_all, key_pos, factor
        )
        dk_all = dk_all + dk_part
        dv_all = dv_all + dv_part
        dq_all = add_rows(dq_all, dq_blk, offset)
        return (dq_all, dk_all, dv_all)

    dq_all, dk_all, dv_all = lax.fori_loop(0, piece_rows // step_rows, one_block, init)
    query_mine = lax.psum_scatter(
        dq_all.reshape(query_len, full_width), "ka", scatter_dimension=0, tiled=True
    )
    query_grad = (query_mine * factor).astype(jnp.bfloat16)
    key_flat = dk_all.reshape(key_len, full_width)
    value_flat = dv_all.reshape(key_len, full_width)
    key_total, value_total = lax.psum((key_flat, value_flat), "pb")
    key_mine = lax.dynamic_slice_in_dim(key_total, index_pb * row_count, row_count, 0)
    value_mine = lax.dynamic_slice_in_dim(value_total, index_pb * row_count, row_count, 0)
    key_grad = (key_mine * factor).astype(jnp.bfloat16)
    value_grad = value_mine.astype(jnp.bfloat16)
    return (query_grad, key_grad, value_grad)


MESH = pl.DeviceIdType.MESH
NT = (((1,), (1,)), ((), ()))
TN = (((0,), (0,)), ((), ()))


def plane_kernel(
    rows, factor,
    q_in, k_in, v_in, o_in, g_in, lse_in, map_in,
    dq_out, dk_out, dv_out,
    q_buf, g_buf, k_buf, v_buf, o_buf, lse_buf, map_buf, stat,
    dq_acc, dk_acc, dv_acc,
    kv_send, kv_recv, dq_send, dq_recv,
    local_sem, send_sem, recv_sem,
):
    p = lax.axis_index("pb")
    x = lax.axis_index("ka")
    h = lax.axis_index("ha")
    c = lax.rem(p, 2)
    y = p // 2
    p_core = p + 1 - 2 * c
    p_far = lax.rem(p + 2, 4)
    to_core = (p_core, x, h)
    to_x = (p, 1 - x, h)
    to_y = (p_far, x, h)
    to_both = (p_core, 1 - x, h)
    fold_rows = rows // 2

    def part(slot):
        return pl.ds(slot * rows, rows)

    barrier = pltpu.get_barrier_semaphore()
    for peer in (to_core, to_x, to_y, to_both):
        pl.semaphore_signal(barrier, inc=1, device_id=peer, device_id_type=MESH)
    locals_ = []
    for n, (src, dst) in enumerate((
        (g_in, g_buf.at[part(0)]), (o_in, o_buf), (lse_in, lse_buf), (q_in, q_buf.at[part(0)]),
        (k_in, k_buf.at[part(0)]), (v_in, v_buf.at[part(0)]), (map_in, map_buf),
    )):
        copy = pltpu.make_async_copy(src, dst, local_sem.at[n])
        copy.start()
        locals_.append(copy)
    pl.semaphore_wait(barrier, 4)

    sends = []

    def send(n, src, dst, peer):
        copy = pltpu.make_async_remote_copy(
            src_ref=src, dst_ref=dst, send_sem=send_sem.at[n], recv_sem=recv_sem.at[n],
            device_id=peer, device_id_type=MESH,
        )
        copy.start()
        sends.append(copy)
        return copy

    q_x = send(0, q_in, q_buf.at[part(2)], to_x)
    k_y = send(1, k_in, k_buf.at[part(1)], to_y)
    q_c = send(2, q_in, q_buf.at[part(1)], to_core)
    g_c = send(3, g_in, g_buf.at[part(1)], to_core)

    for copy in locals_[:3]:
        copy.wait()
    gram = lax.dot_general(o_buf[...], g_buf[part(0)], NT, preferred_element_type=jnp.float32)
    down = lax.broadcasted_iota(jnp.int32, (rows, rows), 0)
    along = lax.broadcasted_iota(jnp.int32, (rows, rows), 1)
    delta = jnp.sum(jnp.where(down == along, gram, 0.0), axis=0, keepdims=True)
    delta = delta.astype(jnp.bfloat16).astype(jnp.float32)
    log2e = math.log2(math.e)
    lse = lse_buf[...].astype(jnp.float32) * log2e
    which = lax.broadcasted_iota(jnp.int32, (8, rows), 0)
    stat[0] = jnp.where(which == 0, lse, delta)
    st_c = send(6, stat.at[0], stat.at[1], to_core)
    st_x = send(7, stat.at[0], stat.at[2], to_x)
    st_b = send(8, stat.at[0], stat.at[3], to_both)
    for copy in locals_[3:]:
        copy.wait()
    q_x.wait_send()
    g_x = send(4, g_in, g_buf.at[part(2)], to_x)
    k_y.wait_send()
    v_y = send(5, v_in, v_buf.at[part(1)], to_y)

    q_owner = (p * 2 + x, p_core * 2 + x, p * 2 + 1 - x, p_core * 2 + 1 - x)
    k_owner = (p * 2 + x, p_far * 2 + x)
    half = lax.broadcasted_iota(jnp.int32, (1, rows), 1) // fold_rows
    lane = lax.broadcasted_iota(jnp.int32, (fold_rows, rows), 1) % fold_rows
    level = lax.broadcasted_iota(jnp.int32, (fold_rows, rows), 0)

    def span(slots):
        return pl.ds(slots[0] * rows, len(slots) * rows)

    def stat_row(n, slots):
        return jnp.concatenate([stat[s, n:n + 1, :] for s in slots], axis=1)

    def probabilities(keyed, asked, scores):
        own = keyed == [0] and asked == [0]
        q_fold = jnp.concatenate([
            jnp.where(half == 0, map_buf[q_owner[s] * 2], map_buf[q_owner[s] * 2 + 1])
            for s in asked], axis=1)
        lse_row = stat_row(0, asked)
        parts = []
        for n in range(2 * len(keyed)):
            k_fold = map_buf[k_owner[keyed[n // 2]] * 2 + n % 2]
            scaled = scores[n * fold_rows:(n + 1) * fold_rows] * (factor * log2e)
            if own:
                seen = k_fold * fold_rows + level <= q_fold * fold_rows + lane
                parts.append(jnp.where(seen, jnp.exp2(scaled - lse_row), 0.0))
            else:
                parts.append(jnp.exp2(scaled - jnp.where(q_fold > k_fold, lse_row, 1e30)))
        return parts

    def score_stage(keyed, asked):
        scores = lax.dot_general(
            k_buf[span(keyed)], q_buf[span(asked)], NT, preferred_element_type=jnp.float32)
        return probabilities(keyed, asked, scores)

    def grad_stage(keyed, asked, parts, first_q, first_k, after_dv=None, after_dk=None):
        query, grad = q_buf[span(asked)], g_buf[span(asked)]
        dprobs = lax.dot_general(v_buf[span(keyed)], grad, NT, preferred_element_type=jnp.float32)
        delta_row = stat_row(1, asked)
        lows = []
        for n in reversed(range(len(keyed))):
            j = keyed[n]
            probs = jnp.concatenate(parts[2 * n:2 * n + 2], axis=0)
            dv = jnp.dot(probs.astype(jnp.bfloat16), grad, preferred_element_type=jnp.float32)
            dv_acc[part(j)] = dv if first_k else dv_acc[part(j)] + dv
            if after_dv is not None and j == 1:
                after_dv()
            dscores = probs * (dprobs[n * rows:(n + 1) * rows] - delta_row)
            lows.insert(0, dscores.astype(jnp.bfloat16))
            dk = jnp.dot(lows[0], query, preferred_element_type=jnp.float32)
            dk_acc[part(j)] = dk if first_k else dk_acc[part(j)] + dk
            if after_dk is not None and j == 1:
                after_dk()
        low = jnp.concatenate(lows, axis=0)
        dq = lax.dot_general(k_buf[span(keyed)], low, TN, preferred_element_type=jnp.float32)
        dq_acc[:, span(asked)] = dq if first_q else dq_acc[:, span(asked)] + dq

    def send_dq(n, s, peer):
        dq_send[s - 1] = dq_acc[:, part(s)].astype(jnp.bfloat16)
        return send(n, dq_send.at[s - 1], dq_recv.at[s - 1], peer)

    def send_kv(n, i, acc):
        kv_send[i] = acc[part(1)].astype(jnp.bfloat16)
        return send(n, kv_send.at[i], kv_recv.at[i], to_y)

    grad_stage([0], [0], score_stage([0], [0]), True, True)
    q_c.wait_recv()
    g_c.wait_recv()
    st_c.wait_recv()
    grad_stage([0], [1], score_stage([0], [1]), True, False)
    q_x.wait_recv()
    q_r = send(9, q_buf.at[part(2)], q_buf.at[part(3)], to_core)
    k_y.wait_recv()
    near = score_stage([1], [0, 1])
    st_x.wait_recv()
    across = score_stage([0, 1], [2])
    g_x.wait_recv()
    g_r = send(10, g_buf.at[part(2)], g_buf.at[part(3)], to_core)
    q_r.wait_recv()
    st_b.wait_recv()
    corner = score_stage([0, 1], [3])
    v_y.wait_recv()
    grad_stage([1], [0, 1], near, False, True)
    dq_1 = send_dq(11, 1, to_core)
    grad_stage([0, 1], [2], across, True, False)
    dq_2 = send_dq(12, 2, to_x)
    g_r.wait_recv()
    late = []
    grad_stage([0, 1], [3], corner, True, False, lambda: late.append(send_kv(13, 0, dv_acc)),
               lambda: late.append(send_kv(14, 1, dk_acc)))
    dq_3 = send_dq(15, 3, to_both)
    dq_1.wait_recv()
    dq_2.wait_recv()
    dq_mine = (dq_acc[:, part(0)] + dq_recv[0].astype(jnp.float32)) + dq_recv[1].astype(jnp.float32)
    late[0].wait_recv()
    dv_out[...] = (dv_acc[part(0)] + kv_recv[0].astype(jnp.float32)).astype(jnp.bfloat16)
    late[1].wait_recv()
    dk_out[...] = (
        (dk_acc[part(0)] + kv_recv[1].astype(jnp.float32)) * factor).astype(jnp.bfloat16)
    dq_3.wait_recv()
    dq_mine = ((dq_mine + dq_recv[2].astype(jnp.float32)) * factor).T
    dq_out[...] = dq_mine.astype(jnp.bfloat16)
    for copy in sends:
        if copy is not q_x and copy is not k_y:
            copy.wait_send()


def store_kernel(dq_in, dk_in, dv_in, dq_out, dk_out, dv_out, sems):
    copies = []
    for n, (src, dst) in enumerate(((dq_in, dq_out), (dk_in, dk_out), (dv_in, dv_out))):
        copy = pltpu.make_async_copy(src, dst, sems.at[n])
        copy.start()
        copies.append(copy)
    for copy in copies:
        copy.wait()


def plane_body(queries, key_rows, value_rows, outputs, out_grad, saved_lse, fold_map):
    rows, width = queries.shape
    factor = 1.0 / math.sqrt(width)
    low, full = jnp.bfloat16, jnp.float32
    grad = jax.ShapeDtypeStruct((rows, width), low)
    arrays = [
        pltpu.with_memory_space_constraint(a, pltpu.HBM)
        for a in (queries, key_rows, value_rows, outputs, out_grad, saved_lse.reshape(1, rows),
                  fold_map)
    ]
    grads = pl.pallas_call(
        functools.partial(plane_kernel, rows, factor),
        out_shape=(pltpu.VMEM((rows, width), low),) * 3,
        in_specs=[pl.BlockSpec(memory_space=pl.ANY)] * 7,
        out_specs=[pl.BlockSpec(memory_space=pltpu.VMEM)] * 3,
        scratch_shapes=[
            pltpu.VMEM((4 * rows, width), low),
            pltpu.VMEM((4 * rows, width), low),
            pltpu.VMEM((2 * rows, width), low),
            pltpu.VMEM((2 * rows, width), low),
            pltpu.VMEM((rows, width), low),
            pltpu.VMEM((1, rows), low),
            pltpu.SMEM(fold_map.shape, jnp.int32),
            pltpu.VMEM((4, 8, rows), full),
            pltpu.VMEM((width, 4 * rows), full),
            pltpu.VMEM((2 * rows, width), full),
            pltpu.VMEM((2 * rows, width), full),
            pltpu.VMEM((2, rows, width), low),
            pltpu.VMEM((2, rows, width), low),
            pltpu.VMEM((3, width, rows), low),
            pltpu.VMEM((3, width, rows), low),
            pltpu.SemaphoreType.DMA((7,)),
            pltpu.SemaphoreType.DMA((16,)),
            pltpu.SemaphoreType.DMA((16,)),
        ],
        compiler_params=pltpu.CompilerParams(
            collective_id=0, has_side_effects=True, vmem_limit_bytes=32 * 2**20
        ),
        cost_estimate=pl.CostEstimate(
            flops=80 * rows * rows * width,
            bytes_accessed=16 * rows * width,
            transcendentals=8 * rows * rows,
        ),
    )(*arrays)
    return pl.pallas_call(
        store_kernel,
        out_shape=(grad, grad, grad),
        in_specs=[pl.BlockSpec(memory_space=pl.ANY)] * 3,
        out_specs=[pl.BlockSpec(memory_space=pl.ANY)] * 3,
        scratch_shapes=[pltpu.SemaphoreType.DMA((3,))],
        compiler_params=pltpu.CompilerParams(vmem_limit_bytes=2**20),
    )(*[pltpu.with_memory_space_constraint(a, pltpu.VMEM) for a in grads])


def solution(mesh):
    plane = mesh.shape["pb"] == 4 and mesh.shape["ka"] == 2
    return jax.shard_map(
        plane_body if plane else body,
        mesh=mesh,
        in_specs=(
            P(("pb", "ka"), "ha"),
            P(("pb", "ka"), "ha"),
            P(("pb", "ka"), "ha"),
            P(("pb", "ka"), "ha"),
            P(("pb", "ka"), "ha"),
            P(("pb", "ka"), "ha"),
            P(),
        ),
        out_specs=(P(("pb", "ka"), "ha"), P(("pb", "ka"), "ha"), P(("pb", "ka"), "ha")),
        check_vma=False,
    )
```

```python
import functools
import math

import jax
import jax.numpy as jnp
from jax import lax
from jax.experimental import pallas as pl
from jax.experimental.pallas import tpu as pltpu
from jax.sharding import PartitionSpec as P


def block_length(row_total):
    length = row_total
    while length > 512 and length % 2 == 0:
        length = length // 2
    return length


def tile_grads(
    query_blk, grad_blk, lse_blk, delta_blk, query_pos, key_blk, value_blk, key_pos, factor
):
    scores = (
        jnp.einsum("qhd,khd->hqk", query_blk, key_blk, preferred_element_type=jnp.float32) * factor
    )
    visible = key_pos[None, :] <= query_pos[:, None]
    probs = jnp.where(visible[None], jnp.exp(scores - lse_blk.T[:, :, None]), 0.0)
    probs_low = probs.astype(jnp.bfloat16)
    value_part = jnp.einsum("hqk,qhd->khd", probs_low, grad_blk, preferred_element_type=jnp.float32)
    dprobs = jnp.einsum("qhd,khd->hqk", grad_blk, value_blk, preferred_element_type=jnp.float32)
    dscores = (probs * (dprobs - delta_blk.T[:, :, None])).astype(jnp.bfloat16)
    query_part = jnp.einsum("hqk,khd->qhd", dscores, key_blk, preferred_element_type=jnp.float32)
    key_part = jnp.einsum("hqk,qhd->khd", dscores, query_blk, preferred_element_type=jnp.float32)
    return (query_part, key_part, value_part)


def add_rows(target, update, first_row):
    length = update.shape[0]
    current = lax.dynamic_slice_in_dim(target, first_row, length, 0)
    return lax.dynamic_update_slice_in_dim(target, current + update, first_row, 0)


def body(queries, key_rows, value_rows, outputs, out_grad, saved_lse, fold_map):
    row_count, full_width = queries.shape
    head_count = saved_lse.shape[1]
    head_dim = full_width // head_count
    factor = 1.0 / math.sqrt(head_dim)
    fold_rows = row_count // 2
    size_pb = lax.axis_size("pb")
    size_ka = lax.axis_size("ka")
    index_pb = lax.axis_index("pb")
    index_ka = lax.axis_index("ka")
    key_all, value_all = (
        lax.all_gather(key_rows, "pb", axis=0, tiled=True),
        lax.all_gather(value_rows, "pb", axis=0, tiled=True),
    )
    key_len = size_pb * row_count
    key_all = key_all.reshape(key_len, head_count, head_dim)
    value_all = value_all.reshape(key_len, head_count, head_dim)
    key_iota = jnp.arange(key_len, dtype=jnp.int32)
    key_global = (key_iota // row_count * size_ka + index_ka) * row_count + key_iota % row_count
    key_pos = fold_map[key_global // fold_rows] * fold_rows + key_global % fold_rows
    query_len = size_ka * row_count
    query_first = index_pb * query_len
    query_empty = jnp.zeros((query_len, head_count, head_dim), jnp.float32)
    key_empty = jnp.zeros((key_len, head_count, head_dim), jnp.float32)
    init = (query_empty, key_empty, key_empty)
    query_src = lax.all_gather(queries, "ka", axis=0, tiled=True)
    grad_src = lax.all_gather(out_grad, "ka", axis=0, tiled=True)
    saved_src = lax.all_gather(outputs, "ka", axis=0, tiled=True)
    lse_src = lax.all_gather(saved_lse, "ka", axis=0, tiled=True)
    piece_rows = query_src.shape[0]
    step_rows = block_length(piece_rows)

    def one_block(number, state):
        dq_all, dk_all, dv_all = state
        offset = number * step_rows
        query_blk = lax.dynamic_slice_in_dim(query_src, offset, step_rows, 0).reshape(
            step_rows, head_count, head_dim
        )
        grad_blk = lax.dynamic_slice_in_dim(grad_src, offset, step_rows, 0).reshape(
            step_rows, head_count, head_dim
        )
        lse_blk = lax.dynamic_slice_in_dim(lse_src, offset, step_rows, 0).astype(jnp.float32)
        saved_blk = lax.dynamic_slice_in_dim(saved_src, offset, step_rows, 0).reshape(
            step_rows, head_count, head_dim
        )
        delta_low = jnp.einsum(
            "qhd,qhd->qh", grad_blk, saved_blk, preferred_element_type=jnp.float32
        ).astype(jnp.bfloat16)
        delta_blk = lax.optimization_barrier(delta_low).astype(jnp.float32)
        row_global = query_first + offset + jnp.arange(step_rows, dtype=jnp.int32)
        query_pos = fold_map[row_global // fold_rows] * fold_rows + row_global % fold_rows
        dq_blk, dk_part, dv_part = tile_grads(
            query_blk, grad_blk, lse_blk, delta_blk, query_pos, key_all, value_all, key_pos, factor
        )
        dk_all = dk_all + dk_part
        dv_all = dv_all + dv_part
        dq_all = add_rows(dq_all, dq_blk, offset)
        return (dq_all, dk_all, dv_all)

    dq_all, dk_all, dv_all = lax.fori_loop(0, piece_rows // step_rows, one_block, init)
    query_mine = lax.psum_scatter(
        dq_all.reshape(query_len, full_width), "ka", scatter_dimension=0, tiled=True
    )
    query_grad = (query_mine * factor).astype(jnp.bfloat16)
    key_flat = dk_all.reshape(key_len, full_width)
    value_flat = dv_all.reshape(key_len, full_width)
    key_total, value_total = lax.psum((key_flat, value_flat), "pb")
    key_mine = lax.dynamic_slice_in_dim(key_total, index_pb * row_count, row_count, 0)
    value_mine = lax.dynamic_slice_in_dim(value_total, index_pb * row_count, row_count, 0)
    key_grad = (key_mine * factor).astype(jnp.bfloat16)
    value_grad = value_mine.astype(jnp.bfloat16)
    return (query_grad, key_grad, value_grad)


MESH = pl.DeviceIdType.MESH
NT = (((1,), (1,)), ((), ()))
TN = (((0,), (0,)), ((), ()))


def plane_kernel(
    rows, factor,
    q_in, k_in, v_in, o_in, g_in, lse_in, map_in,
    dq_out, dk_out, dv_out,
    q_buf, g_buf, k_buf, v_buf, o_buf, lse_buf, map_buf, stat,
    dq_acc, dk_acc, dv_acc,
    kv_send, kv_recv, dq_send, dq_recv,
    local_sem, send_sem, recv_sem,
):
    p = lax.axis_index("pb")
    x = lax.axis_index("ka")
    h = lax.axis_index("ha")
    c = lax.rem(p, 2)
    y = p // 2
    p_core = p + 1 - 2 * c
    p_far = lax.rem(p + 2, 4)
    to_core = (p_core, x, h)
    to_x = (p, 1 - x, h)
    to_y = (p_far, x, h)
    to_both = (p_core, 1 - x, h)
    fold_rows = rows // 2

    def part(slot):
        return pl.ds(slot * rows, rows)

    barrier = pltpu.get_barrier_semaphore()
    for peer in (to_core, to_x, to_y, to_both):
        pl.semaphore_signal(barrier, inc=1, device_id=peer, device_id_type=MESH)
    locals_ = []
    for n, (src, dst) in enumerate((
        (g_in, g_buf.at[part(0)]), (o_in, o_buf), (lse_in, lse_buf), (q_in, q_buf.at[part(0)]),
        (k_in, k_buf.at[part(0)]), (v_in, v_buf.at[part(0)]), (map_in, map_buf),
    )):
        copy = pltpu.make_async_copy(src, dst, local_sem.at[n])
        copy.start()
        locals_.append(copy)
    pl.semaphore_wait(barrier, 4)

    sends = []

    def send(n, src, dst, peer):
        copy = pltpu.make_async_remote_copy(
            src_ref=src, dst_ref=dst, send_sem=send_sem.at[n], recv_sem=recv_sem.at[n],
            device_id=peer, device_id_type=MESH,
        )
        copy.start()
        sends.append(copy)
        return copy

    q_x = send(0, q_in, q_buf.at[part(2)], to_x)
    k_y = send(1, k_in, k_buf.at[part(1)], to_y)
    q_c = send(2, q_in, q_buf.at[part(1)], to_core)
    g_c = send(3, g_in, g_buf.at[part(1)], to_core)
    g_x = send(4, g_in, g_buf.at[part(2)], to_x)
    v_y = send(5, v_in, v_buf.at[part(1)], to_y)

    for copy in locals_[:3]:
        copy.wait()
    gram = lax.dot_general(o_buf[...], g_buf[part(0)], NT, preferred_element_type=jnp.float32)
    down = lax.broadcasted_iota(jnp.int32, (rows, rows), 0)
    along = lax.broadcasted_iota(jnp.int32, (rows, rows), 1)
    delta = jnp.sum(jnp.where(down == along, gram, 0.0), axis=0, keepdims=True)
    delta = delta.astype(jnp.bfloat16).astype(jnp.float32)
    log2e = math.log2(math.e)
    lse = lse_buf[...].astype(jnp.float32) * log2e
    which = lax.broadcasted_iota(jnp.int32, (8, rows), 0)
    stat[0] = jnp.where(which == 0, lse, delta)
    st_c = send(6, stat.at[0], stat.at[1], to_core)
    st_x = send(7, stat.at[0], stat.at[2], to_x)
    st_b = send(8, stat.at[0], stat.at[3], to_both)
    for copy in locals_[3:]:
        copy.wait()

    q_owner = (p * 2 + x, p_core * 2 + x, p * 2 + 1 - x, p_core * 2 + 1 - x)
    k_owner = (p * 2 + x, p_far * 2 + x)
    half = lax.broadcasted_iota(jnp.int32, (1, rows), 1) // fold_rows
    lane = lax.broadcasted_iota(jnp.int32, (fold_rows, rows), 1) % fold_rows
    level = lax.broadcasted_iota(jnp.int32, (fold_rows, rows), 0)

    def span(slots):
        return pl.ds(slots[0] * rows, len(slots) * rows)

    def stat_row(n, slots):
        return jnp.concatenate([stat[s, n:n + 1, :] for s in slots], axis=1)

    def probabilities(keyed, asked, scores):
        own = keyed == [0] and asked == [0]
        q_fold = jnp.concatenate([
            jnp.where(half == 0, map_buf[q_owner[s] * 2], map_buf[q_owner[s] * 2 + 1])
            for s in asked], axis=1)
        lse_row = stat_row(0, asked)
        parts = []
        for n in range(2 * len(keyed)):
            k_fold = map_buf[k_owner[keyed[n // 2]] * 2 + n % 2]
            scaled = scores[n * fold_rows:(n + 1) * fold_rows] * (factor * log2e)
            if own:
                seen = k_fold * fold_rows + level <= q_fold * fold_rows + lane
                parts.append(jnp.where(seen, jnp.exp2(scaled - lse_row), 0.0))
            else:
                parts.append(jnp.exp2(scaled - jnp.where(q_fold > k_fold, lse_row, 1e30)))
        return parts

    def tile(keyed, asked, first_q, first_k, after_dv=None, after_dk=None):
        query, grad = q_buf[span(asked)], g_buf[span(asked)]
        scores = lax.dot_general(k_buf[span(keyed)], query, NT, preferred_element_type=jnp.float32)
        dprobs = lax.dot_general(v_buf[span(keyed)], grad, NT, preferred_element_type=jnp.float32)
        parts = probabilities(keyed, asked, scores)
        delta_row = stat_row(1, asked)
        lows = []
        for n in reversed(range(len(keyed))):
            j = keyed[n]
            probs = jnp.concatenate(parts[2 * n:2 * n + 2], axis=0)
            dv = jnp.dot(probs.astype(jnp.bfloat16), grad, preferred_element_type=jnp.float32)
            dv_acc[part(j)] = dv if first_k else dv_acc[part(j)] + dv
            if after_dv is not None and j == 1:
                after_dv()
            dscores = probs * (dprobs[n * rows:(n + 1) * rows] - delta_row)
            lows.insert(0, dscores.astype(jnp.bfloat16))
            dk = jnp.dot(lows[0], query, preferred_element_type=jnp.float32)
            dk_acc[part(j)] = dk if first_k else dk_acc[part(j)] + dk
            if after_dk is not None and j == 1:
                after_dk()
        low = jnp.concatenate(lows, axis=0)
        dq = lax.dot_general(k_buf[span(keyed)], low, TN, preferred_element_type=jnp.float32)
        dq_acc[:, span(asked)] = dq if first_q else dq_acc[:, span(asked)] + dq

    def send_dq(n, s, peer):
        dq_send[s - 1] = dq_acc[:, part(s)].astype(jnp.bfloat16)
        return send(n, dq_send.at[s - 1], dq_recv.at[s - 1], peer)

    def send_kv(n, i, acc):
        kv_send[i] = acc[part(1)].astype(jnp.bfloat16)
        return send(n, kv_send.at[i], kv_recv.at[i], to_y)

    tile([0], [0], True, True)
    q_x.wait_recv()
    q_r = send(9, q_buf.at[part(2)], q_buf.at[part(3)], to_core)
    g_x.wait_recv()
    g_r = send(10, g_buf.at[part(2)], g_buf.at[part(3)], to_core)
    q_c.wait_recv()
    g_c.wait_recv()
    st_c.wait_recv()
    tile([0], [1], True, False)
    k_y.wait_recv()
    v_y.wait_recv()
    tile([1], [0, 1], False, True)
    dq_1 = send_dq(11, 1, to_core)
    st_x.wait_recv()
    tile([0, 1], [2], True, False)
    dq_2 = send_dq(12, 2, to_x)
    q_r.wait_recv()
    g_r.wait_recv()
    st_b.wait_recv()
    late = []
    tile([0, 1], [3], True, False, lambda: late.append(send_kv(13, 0, dv_acc)),
         lambda: late.append(send_kv(14, 1, dk_acc)))
    dq_3 = send_dq(15, 3, to_both)
    dq_1.wait_recv()
    dq_2.wait_recv()
    dq_mine = (dq_acc[:, part(0)] + dq_recv[0].astype(jnp.float32)) + dq_recv[1].astype(jnp.float32)
    late[0].wait_recv()
    dv_out[...] = (dv_acc[part(0)] + kv_recv[0].astype(jnp.float32)).astype(jnp.bfloat16)
    late[1].wait_recv()
    dk_out[...] = (
        (dk_acc[part(0)] + kv_recv[1].astype(jnp.float32)) * factor).astype(jnp.bfloat16)
    dq_3.wait_recv()
    dq_mine = ((dq_mine + dq_recv[2].astype(jnp.float32)) * factor).T
    dq_out[...] = dq_mine.astype(jnp.bfloat16)
    for copy in sends:
        copy.wait_send()


def store_kernel(dq_in, dk_in, dv_in, dq_out, dk_out, dv_out, sems):
    copies = []
    for n, (src, dst) in enumerate(((dq_in, dq_out), (dk_in, dk_out), (dv_in, dv_out))):
        copy = pltpu.make_async_copy(src, dst, sems.at[n])
        copy.start()
        copies.append(copy)
    for copy in copies:
        copy.wait()


def plane_body(queries, key_rows, value_rows, outputs, out_grad, saved_lse, fold_map):
    rows, width = queries.shape
    factor = 1.0 / math.sqrt(width)
    low, full = jnp.bfloat16, jnp.float32
    grad = jax.ShapeDtypeStruct((rows, width), low)
    arrays = [
        pltpu.with_memory_space_constraint(a, pltpu.HBM)
        for a in (queries, key_rows, value_rows, outputs, out_grad, saved_lse.reshape(1, rows),
                  fold_map)
    ]
    grads = pl.pallas_call(
        functools.partial(plane_kernel, rows, factor),
        out_shape=(pltpu.VMEM((rows, width), low),) * 3,
        in_specs=[pl.BlockSpec(memory_space=pl.ANY)] * 7,
        out_specs=[pl.BlockSpec(memory_space=pltpu.VMEM)] * 3,
        scratch_shapes=[
            pltpu.VMEM((4 * rows, width), low),
            pltpu.VMEM((4 * rows, width), low),
            pltpu.VMEM((2 * rows, width), low),
            pltpu.VMEM((2 * rows, width), low),
            pltpu.VMEM((rows, width), low),
            pltpu.VMEM((1, rows), low),
            pltpu.SMEM(fold_map.shape, jnp.int32),
            pltpu.VMEM((4, 8, rows), full),
            pltpu.VMEM((width, 4 * rows), full),
            pltpu.VMEM((2 * rows, width), full),
            pltpu.VMEM((2 * rows, width), full),
            pltpu.VMEM((2, rows, width), low),
            pltpu.VMEM((2, rows, width), low),
            pltpu.VMEM((3, width, rows), low),
            pltpu.VMEM((3, width, rows), low),
            pltpu.SemaphoreType.DMA((7,)),
            pltpu.SemaphoreType.DMA((16,)),
            pltpu.SemaphoreType.DMA((16,)),
        ],
        compiler_params=pltpu.CompilerParams(
            collective_id=0, has_side_effects=True, vmem_limit_bytes=32 * 2**20
        ),
        cost_estimate=pl.CostEstimate(
            flops=80 * rows * rows * width,
            bytes_accessed=16 * rows * width,
            transcendentals=8 * rows * rows,
        ),
    )(*arrays)
    return pl.pallas_call(
        store_kernel,
        out_shape=(grad, grad, grad),
        in_specs=[pl.BlockSpec(memory_space=pl.ANY)] * 3,
        out_specs=[pl.BlockSpec(memory_space=pl.ANY)] * 3,
        scratch_shapes=[pltpu.SemaphoreType.DMA((3,))],
        compiler_params=pltpu.CompilerParams(vmem_limit_bytes=2**20),
    )(*[pltpu.with_memory_space_constraint(a, pltpu.VMEM) for a in grads])


def solution(mesh):
    plane = mesh.shape["pb"] == 4 and mesh.shape["ka"] == 2
    return jax.shard_map(
        plane_body if plane else body,
        mesh=mesh,
        in_specs=(
            P(("pb", "ka"), "ha"),
            P(("pb", "ka"), "ha"),
            P(("pb", "ka"), "ha"),
            P(("pb", "ka"), "ha"),
            P(("pb", "ka"), "ha"),
            P(("pb", "ka"), "ha"),
            P(),
        ),
        out_specs=(P(("pb", "ka"), "ha"), P(("pb", "ka"), "ha"), P(("pb", "ka"), "ha")),
        check_vma=False,
    )
```

```python
import functools
import math

import jax
import jax.numpy as jnp
from jax import lax
from jax.experimental import pallas as pl
from jax.experimental.pallas import tpu as pltpu
from jax.sharding import PartitionSpec as P


def block_length(row_total):
    length = row_total
    while length > 512 and length % 2 == 0:
        length = length // 2
    return length


def tile_grads(
    query_blk, grad_blk, lse_blk, delta_blk, query_pos, key_blk, value_blk, key_pos, factor
):
    scores = (
        jnp.einsum("qhd,khd->hqk", query_blk, key_blk, preferred_element_type=jnp.float32) * factor
    )
    visible = key_pos[None, :] <= query_pos[:, None]
    probs = jnp.where(visible[None], jnp.exp(scores - lse_blk.T[:, :, None]), 0.0)
    probs_low = probs.astype(jnp.bfloat16)
    value_part = jnp.einsum("hqk,qhd->khd", probs_low, grad_blk, preferred_element_type=jnp.float32)
    dprobs = jnp.einsum("qhd,khd->hqk", grad_blk, value_blk, preferred_element_type=jnp.float32)
    dscores = (probs * (dprobs - delta_blk.T[:, :, None])).astype(jnp.bfloat16)
    query_part = jnp.einsum("hqk,khd->qhd", dscores, key_blk, preferred_element_type=jnp.float32)
    key_part = jnp.einsum("hqk,qhd->khd", dscores, query_blk, preferred_element_type=jnp.float32)
    return (query_part, key_part, value_part)


def add_rows(target, update, first_row):
    length = update.shape[0]
    current = lax.dynamic_slice_in_dim(target, first_row, length, 0)
    return lax.dynamic_update_slice_in_dim(target, current + update, first_row, 0)


def body(queries, key_rows, value_rows, outputs, out_grad, saved_lse, fold_map):
    row_count, full_width = queries.shape
    head_count = saved_lse.shape[1]
    head_dim = full_width // head_count
    factor = 1.0 / math.sqrt(head_dim)
    fold_rows = row_count // 2
    size_pb = lax.axis_size("pb")
    size_ka = lax.axis_size("ka")
    index_pb = lax.axis_index("pb")
    index_ka = lax.axis_index("ka")
    key_all, value_all = (
        lax.all_gather(key_rows, "pb", axis=0, tiled=True),
        lax.all_gather(value_rows, "pb", axis=0, tiled=True),
    )
    key_len = size_pb * row_count
    key_all = key_all.reshape(key_len, head_count, head_dim)
    value_all = value_all.reshape(key_len, head_count, head_dim)
    key_iota = jnp.arange(key_len, dtype=jnp.int32)
    key_global = (key_iota // row_count * size_ka + index_ka) * row_count + key_iota % row_count
    key_pos = fold_map[key_global // fold_rows] * fold_rows + key_global % fold_rows
    query_len = size_ka * row_count
    query_first = index_pb * query_len
    query_empty = jnp.zeros((query_len, head_count, head_dim), jnp.float32)
    key_empty = jnp.zeros((key_len, head_count, head_dim), jnp.float32)
    init = (query_empty, key_empty, key_empty)
    query_src = lax.all_gather(queries, "ka", axis=0, tiled=True)
    grad_src = lax.all_gather(out_grad, "ka", axis=0, tiled=True)
    saved_src = lax.all_gather(outputs, "ka", axis=0, tiled=True)
    lse_src = lax.all_gather(saved_lse, "ka", axis=0, tiled=True)
    piece_rows = query_src.shape[0]
    step_rows = block_length(piece_rows)

    def one_block(number, state):
        dq_all, dk_all, dv_all = state
        offset = number * step_rows
        query_blk = lax.dynamic_slice_in_dim(query_src, offset, step_rows, 0).reshape(
            step_rows, head_count, head_dim
        )
        grad_blk = lax.dynamic_slice_in_dim(grad_src, offset, step_rows, 0).reshape(
            step_rows, head_count, head_dim
        )
        lse_blk = lax.dynamic_slice_in_dim(lse_src, offset, step_rows, 0).astype(jnp.float32)
        saved_blk = lax.dynamic_slice_in_dim(saved_src, offset, step_rows, 0).reshape(
            step_rows, head_count, head_dim
        )
        delta_low = jnp.einsum(
            "qhd,qhd->qh", grad_blk, saved_blk, preferred_element_type=jnp.float32
        ).astype(jnp.bfloat16)
        delta_blk = lax.optimization_barrier(delta_low).astype(jnp.float32)
        row_global = query_first + offset + jnp.arange(step_rows, dtype=jnp.int32)
        query_pos = fold_map[row_global // fold_rows] * fold_rows + row_global % fold_rows
        dq_blk, dk_part, dv_part = tile_grads(
            query_blk, grad_blk, lse_blk, delta_blk, query_pos, key_all, value_all, key_pos, factor
        )
        dk_all = dk_all + dk_part
        dv_all = dv_all + dv_part
        dq_all = add_rows(dq_all, dq_blk, offset)
        return (dq_all, dk_all, dv_all)

    dq_all, dk_all, dv_all = lax.fori_loop(0, piece_rows // step_rows, one_block, init)
    query_mine = lax.psum_scatter(
        dq_all.reshape(query_len, full_width), "ka", scatter_dimension=0, tiled=True
    )
    query_grad = (query_mine * factor).astype(jnp.bfloat16)
    key_flat = dk_all.reshape(key_len, full_width)
    value_flat = dv_all.reshape(key_len, full_width)
    key_total, value_total = lax.psum((key_flat, value_flat), "pb")
    key_mine = lax.dynamic_slice_in_dim(key_total, index_pb * row_count, row_count, 0)
    value_mine = lax.dynamic_slice_in_dim(value_total, index_pb * row_count, row_count, 0)
    key_grad = (key_mine * factor).astype(jnp.bfloat16)
    value_grad = value_mine.astype(jnp.bfloat16)
    return (query_grad, key_grad, value_grad)


MESH = pl.DeviceIdType.MESH
NT = (((1,), (1,)), ((), ()))
TN = (((0,), (0,)), ((), ()))


def plane_kernel(
    rows, factor,
    q_in, k_in, v_in, o_in, g_in, lse_in, map_in,
    dq_out, dk_out, dv_out,
    q_buf, g_buf, k_buf, v_buf, o_buf, lse_buf, map_buf, stat,
    dq_acc, dk_acc, dv_acc,
    kv_send, kv_recv, dq_send, dq_recv,
    local_sem, send_sem, recv_sem,
):
    p = lax.axis_index("pb")
    x = lax.axis_index("ka")
    h = lax.axis_index("ha")
    c = lax.rem(p, 2)
    y = p // 2
    p_core = p + 1 - 2 * c
    p_far = lax.rem(p + 2, 4)
    to_core = (p_core, x, h)
    to_x = (p, 1 - x, h)
    to_y = (p_far, x, h)
    to_both = (p_core, 1 - x, h)
    fold_rows = rows // 2

    def part(slot):
        return pl.ds(slot * rows, rows)

    barrier = pltpu.get_barrier_semaphore()
    for peer in (to_core, to_x, to_y, to_both):
        pl.semaphore_signal(barrier, inc=1, device_id=peer, device_id_type=MESH)
    locals_ = []
    for n, (src, dst) in enumerate((
        (g_in, g_buf.at[part(0)]), (o_in, o_buf), (lse_in, lse_buf), (q_in, q_buf.at[part(0)]),
        (k_in, k_buf.at[part(0)]), (v_in, v_buf.at[part(0)]), (map_in, map_buf),
    )):
        copy = pltpu.make_async_copy(src, dst, local_sem.at[n])
        copy.start()
        locals_.append(copy)
    pl.semaphore_wait(barrier, 4)

    sends = []

    def send(n, src, dst, peer):
        copy = pltpu.make_async_remote_copy(
            src_ref=src, dst_ref=dst, send_sem=send_sem.at[n], recv_sem=recv_sem.at[n],
            device_id=peer, device_id_type=MESH,
        )
        copy.start()
        sends.append(copy)
        return copy

    q_x = send(0, q_in, q_buf.at[part(2)], to_x)
    k_y = send(1, k_in, k_buf.at[part(1)], to_y)
    q_c = send(2, q_in, q_buf.at[part(1)], to_core)
    g_c = send(3, g_in, g_buf.at[part(1)], to_core)
    g_x = send(4, g_in, g_buf.at[part(2)], to_x)
    v_y = send(5, v_in, v_buf.at[part(1)], to_y)

    for copy in locals_[:3]:
        copy.wait()
    gram = lax.dot_general(o_buf[...], g_buf[part(0)], NT, preferred_element_type=jnp.float32)
    down = lax.broadcasted_iota(jnp.int32, (rows, rows), 0)
    along = lax.broadcasted_iota(jnp.int32, (rows, rows), 1)
    delta = jnp.sum(jnp.where(down == along, gram, 0.0), axis=0, keepdims=True)
    delta = delta.astype(jnp.bfloat16).astype(jnp.float32)
    log2e = math.log2(math.e)
    lse = lse_buf[...].astype(jnp.float32) * log2e
    which = lax.broadcasted_iota(jnp.int32, (8, rows), 0)
    stat[0] = jnp.where(which == 0, lse, delta)
    st_c = send(6, stat.at[0], stat.at[1], to_core)
    st_x = send(7, stat.at[0], stat.at[2], to_x)
    st_b = send(8, stat.at[0], stat.at[3], to_both)
    for copy in locals_[3:]:
        copy.wait()

    q_owner = (p * 2 + x, p_core * 2 + x, p * 2 + 1 - x, p_core * 2 + 1 - x)
    k_owner = (p * 2 + x, p_far * 2 + x)
    half = lax.broadcasted_iota(jnp.int32, (1, rows), 1) // fold_rows
    lane = lax.broadcasted_iota(jnp.int32, (fold_rows, rows), 1) % fold_rows
    level = lax.broadcasted_iota(jnp.int32, (fold_rows, rows), 0)

    def span(slots):
        return pl.ds(slots[0] * rows, len(slots) * rows)

    def stat_row(n, slots):
        return jnp.concatenate([stat[s, n:n + 1, :] for s in slots], axis=1)

    def probabilities(keyed, asked, scores):
        own = keyed == [0] and asked == [0]
        q_fold = jnp.concatenate([
            jnp.where(half == 0, map_buf[q_owner[s] * 2], map_buf[q_owner[s] * 2 + 1])
            for s in asked], axis=1)
        lse_row = stat_row(0, asked)
        parts = []
        for n in range(2 * len(keyed)):
            k_fold = map_buf[k_owner[keyed[n // 2]] * 2 + n % 2]
            scaled = scores[n * fold_rows:(n + 1) * fold_rows] * (factor * log2e)
            if own:
                seen = k_fold * fold_rows + level <= q_fold * fold_rows + lane
                parts.append(jnp.where(seen, jnp.exp2(scaled - lse_row), 0.0))
            else:
                parts.append(jnp.exp2(scaled - jnp.where(q_fold > k_fold, lse_row, 1e30)))
        return parts

    def tile(keyed, asked, first_q, first_k, after_dv=None, after_dk=None):
        query, grad = q_buf[span(asked)], g_buf[span(asked)]
        scores = lax.dot_general(k_buf[span(keyed)], query, NT, preferred_element_type=jnp.float32)
        dprobs = lax.dot_general(v_buf[span(keyed)], grad, NT, preferred_element_type=jnp.float32)
        parts = probabilities(keyed, asked, scores)
        delta_row = stat_row(1, asked)
        lows = []
        for n in reversed(range(len(keyed))):
            j = keyed[n]
            probs = jnp.concatenate(parts[2 * n:2 * n + 2], axis=0)
            dv = jnp.dot(probs.astype(jnp.bfloat16), grad, preferred_element_type=jnp.float32)
            dv_acc[part(j)] = dv if first_k else dv_acc[part(j)] + dv
            if after_dv is not None and j == 1:
                after_dv()
            dscores = probs * (dprobs[n * rows:(n + 1) * rows] - delta_row)
            lows.insert(0, dscores.astype(jnp.bfloat16))
            dk = jnp.dot(lows[0], query, preferred_element_type=jnp.float32)
            dk_acc[part(j)] = dk if first_k else dk_acc[part(j)] + dk
            if after_dk is not None and j == 1:
                after_dk()
        low = jnp.concatenate(lows, axis=0)
        dq = lax.dot_general(low, k_buf[span(keyed)], TN, preferred_element_type=jnp.float32)
        dq_acc[span(asked)] = dq if first_q else dq_acc[span(asked)] + dq

    def send_dq(n, s, peer):
        dq_send[s - 1] = dq_acc[part(s)].astype(jnp.bfloat16)
        return send(n, dq_send.at[s - 1], dq_recv.at[s - 1], peer)

    def send_kv(n, i, acc):
        kv_send[i] = acc[part(1)].astype(jnp.bfloat16)
        return send(n, kv_send.at[i], kv_recv.at[i], to_y)

    tile([0], [0], True, True)
    q_x.wait_recv()
    q_r = send(9, q_buf.at[part(2)], q_buf.at[part(3)], to_core)
    g_x.wait_recv()
    g_r = send(10, g_buf.at[part(2)], g_buf.at[part(3)], to_core)
    q_c.wait_recv()
    g_c.wait_recv()
    st_c.wait_recv()
    tile([0], [1], True, False)
    k_y.wait_recv()
    v_y.wait_recv()
    tile([1], [0, 1], False, True)
    dq_1 = send_dq(11, 1, to_core)
    st_x.wait_recv()
    tile([0, 1], [2], True, False)
    dq_2 = send_dq(12, 2, to_x)
    q_r.wait_recv()
    g_r.wait_recv()
    st_b.wait_recv()
    late = []
    tile([1], [3], True, False, lambda: late.append(send_kv(13, 0, dv_acc)),
         lambda: late.append(send_kv(14, 1, dk_acc)))
    tile([0], [3], False, False)
    dq_3 = send_dq(15, 3, to_both)
    dq_1.wait_recv()
    dq_2.wait_recv()
    dq_mine = (dq_acc[part(0)] + dq_recv[0].astype(jnp.float32)) + dq_recv[1].astype(jnp.float32)
    late[0].wait_recv()
    dv_out[...] = (dv_acc[part(0)] + kv_recv[0].astype(jnp.float32)).astype(jnp.bfloat16)
    late[1].wait_recv()
    dk_out[...] = (
        (dk_acc[part(0)] + kv_recv[1].astype(jnp.float32)) * factor).astype(jnp.bfloat16)
    dq_3.wait_recv()
    dq_out[...] = ((dq_mine + dq_recv[2].astype(jnp.float32)) * factor).astype(jnp.bfloat16)
    for copy in sends:
        copy.wait_send()


def store_kernel(dq_in, dk_in, dv_in, dq_out, dk_out, dv_out, sems):
    copies = []
    for n, (src, dst) in enumerate(((dq_in, dq_out), (dk_in, dk_out), (dv_in, dv_out))):
        copy = pltpu.make_async_copy(src, dst, sems.at[n])
        copy.start()
        copies.append(copy)
    for copy in copies:
        copy.wait()


def plane_body(queries, key_rows, value_rows, outputs, out_grad, saved_lse, fold_map):
    rows, width = queries.shape
    factor = 1.0 / math.sqrt(width)
    low, full = jnp.bfloat16, jnp.float32
    grad = jax.ShapeDtypeStruct((rows, width), low)
    arrays = [
        pltpu.with_memory_space_constraint(a, pltpu.HBM)
        for a in (queries, key_rows, value_rows, outputs, out_grad, saved_lse.reshape(1, rows),
                  fold_map)
    ]
    grads = pl.pallas_call(
        functools.partial(plane_kernel, rows, factor),
        out_shape=(pltpu.VMEM((rows, width), low),) * 3,
        in_specs=[pl.BlockSpec(memory_space=pl.ANY)] * 7,
        out_specs=[pl.BlockSpec(memory_space=pltpu.VMEM)] * 3,
        scratch_shapes=[
            pltpu.VMEM((4 * rows, width), low),
            pltpu.VMEM((4 * rows, width), low),
            pltpu.VMEM((2 * rows, width), low),
            pltpu.VMEM((2 * rows, width), low),
            pltpu.VMEM((rows, width), low),
            pltpu.VMEM((1, rows), low),
            pltpu.SMEM(fold_map.shape, jnp.int32),
            pltpu.VMEM((4, 8, rows), full),
            pltpu.VMEM((4 * rows, width), full),
            pltpu.VMEM((2 * rows, width), full),
            pltpu.VMEM((2 * rows, width), full),
            pltpu.VMEM((2, rows, width), low),
            pltpu.VMEM((2, rows, width), low),
            pltpu.VMEM((3, rows, width), low),
            pltpu.VMEM((3, rows, width), low),
            pltpu.SemaphoreType.DMA((7,)),
            pltpu.SemaphoreType.DMA((16,)),
            pltpu.SemaphoreType.DMA((16,)),
        ],
        compiler_params=pltpu.CompilerParams(
            collective_id=0, has_side_effects=True, vmem_limit_bytes=32 * 2**20
        ),
        cost_estimate=pl.CostEstimate(
            flops=80 * rows * rows * width,
            bytes_accessed=16 * rows * width,
            transcendentals=8 * rows * rows,
        ),
    )(*arrays)
    return pl.pallas_call(
        store_kernel,
        out_shape=(grad, grad, grad),
        in_specs=[pl.BlockSpec(memory_space=pl.ANY)] * 3,
        out_specs=[pl.BlockSpec(memory_space=pl.ANY)] * 3,
        scratch_shapes=[pltpu.SemaphoreType.DMA((3,))],
        compiler_params=pltpu.CompilerParams(vmem_limit_bytes=2**20),
    )(*[pltpu.with_memory_space_constraint(a, pltpu.VMEM) for a in grads])


def solution(mesh):
    plane = mesh.shape["pb"] == 4 and mesh.shape["ka"] == 2
    return jax.shard_map(
        plane_body if plane else body,
        mesh=mesh,
        in_specs=(
            P(("pb", "ka"), "ha"),
            P(("pb", "ka"), "ha"),
            P(("pb", "ka"), "ha"),
            P(("pb", "ka"), "ha"),
            P(("pb", "ka"), "ha"),
            P(("pb", "ka"), "ha"),
            P(),
        ),
        out_specs=(P(("pb", "ka"), "ha"), P(("pb", "ka"), "ha"), P(("pb", "ka"), "ha")),
        check_vma=False,
    )
```

```python
import functools
import math

import jax
import jax.numpy as jnp
from jax import lax
from jax.experimental import pallas as pl
from jax.experimental.pallas import tpu as pltpu
from jax.sharding import PartitionSpec as P


def block_length(row_total):
    length = row_total
    while length > 512 and length % 2 == 0:
        length = length // 2
    return length


def tile_grads(
    query_blk, grad_blk, lse_blk, delta_blk, query_pos, key_blk, value_blk, key_pos, factor
):
    scores = (
        jnp.einsum("qhd,khd->hqk", query_blk, key_blk, preferred_element_type=jnp.float32) * factor
    )
    visible = key_pos[None, :] <= query_pos[:, None]
    probs = jnp.where(visible[None], jnp.exp(scores - lse_blk.T[:, :, None]), 0.0)
    probs_low = probs.astype(jnp.bfloat16)
    value_part = jnp.einsum("hqk,qhd->khd", probs_low, grad_blk, preferred_element_type=jnp.float32)
    dprobs = jnp.einsum("qhd,khd->hqk", grad_blk, value_blk, preferred_element_type=jnp.float32)
    dscores = (probs * (dprobs - delta_blk.T[:, :, None])).astype(jnp.bfloat16)
    query_part = jnp.einsum("hqk,khd->qhd", dscores, key_blk, preferred_element_type=jnp.float32)
    key_part = jnp.einsum("hqk,qhd->khd", dscores, query_blk, preferred_element_type=jnp.float32)
    return (query_part, key_part, value_part)


def add_rows(target, update, first_row):
    length = update.shape[0]
    current = lax.dynamic_slice_in_dim(target, first_row, length, 0)
    return lax.dynamic_update_slice_in_dim(target, current + update, first_row, 0)


def body(queries, key_rows, value_rows, outputs, out_grad, saved_lse, fold_map):
    row_count, full_width = queries.shape
    head_count = saved_lse.shape[1]
    head_dim = full_width // head_count
    factor = 1.0 / math.sqrt(head_dim)
    fold_rows = row_count // 2
    size_pb = lax.axis_size("pb")
    size_ka = lax.axis_size("ka")
    index_pb = lax.axis_index("pb")
    index_ka = lax.axis_index("ka")
    key_all, value_all = (
        lax.all_gather(key_rows, "pb", axis=0, tiled=True),
        lax.all_gather(value_rows, "pb", axis=0, tiled=True),
    )
    key_len = size_pb * row_count
    key_all = key_all.reshape(key_len, head_count, head_dim)
    value_all = value_all.reshape(key_len, head_count, head_dim)
    key_iota = jnp.arange(key_len, dtype=jnp.int32)
    key_global = (key_iota // row_count * size_ka + index_ka) * row_count + key_iota % row_count
    key_pos = fold_map[key_global // fold_rows] * fold_rows + key_global % fold_rows
    query_len = size_ka * row_count
    query_first = index_pb * query_len
    query_empty = jnp.zeros((query_len, head_count, head_dim), jnp.float32)
    key_empty = jnp.zeros((key_len, head_count, head_dim), jnp.float32)
    init = (query_empty, key_empty, key_empty)
    query_src = lax.all_gather(queries, "ka", axis=0, tiled=True)
    grad_src = lax.all_gather(out_grad, "ka", axis=0, tiled=True)
    saved_src = lax.all_gather(outputs, "ka", axis=0, tiled=True)
    lse_src = lax.all_gather(saved_lse, "ka", axis=0, tiled=True)
    piece_rows = query_src.shape[0]
    step_rows = block_length(piece_rows)

    def one_block(number, state):
        dq_all, dk_all, dv_all = state
        offset = number * step_rows
        query_blk = lax.dynamic_slice_in_dim(query_src, offset, step_rows, 0).reshape(
            step_rows, head_count, head_dim
        )
        grad_blk = lax.dynamic_slice_in_dim(grad_src, offset, step_rows, 0).reshape(
            step_rows, head_count, head_dim
        )
        lse_blk = lax.dynamic_slice_in_dim(lse_src, offset, step_rows, 0).astype(jnp.float32)
        saved_blk = lax.dynamic_slice_in_dim(saved_src, offset, step_rows, 0).reshape(
            step_rows, head_count, head_dim
        )
        delta_low = jnp.einsum(
            "qhd,qhd->qh", grad_blk, saved_blk, preferred_element_type=jnp.float32
        ).astype(jnp.bfloat16)
        delta_blk = lax.optimization_barrier(delta_low).astype(jnp.float32)
        row_global = query_first + offset + jnp.arange(step_rows, dtype=jnp.int32)
        query_pos = fold_map[row_global // fold_rows] * fold_rows + row_global % fold_rows
        dq_blk, dk_part, dv_part = tile_grads(
            query_blk, grad_blk, lse_blk, delta_blk, query_pos, key_all, value_all, key_pos, factor
        )
        dk_all = dk_all + dk_part
        dv_all = dv_all + dv_part
        dq_all = add_rows(dq_all, dq_blk, offset)
        return (dq_all, dk_all, dv_all)

    dq_all, dk_all, dv_all = lax.fori_loop(0, piece_rows // step_rows, one_block, init)
    query_mine = lax.psum_scatter(
        dq_all.reshape(query_len, full_width), "ka", scatter_dimension=0, tiled=True
    )
    query_grad = (query_mine * factor).astype(jnp.bfloat16)
    key_flat = dk_all.reshape(key_len, full_width)
    value_flat = dv_all.reshape(key_len, full_width)
    key_total, value_total = lax.psum((key_flat, value_flat), "pb")
    key_mine = lax.dynamic_slice_in_dim(key_total, index_pb * row_count, row_count, 0)
    value_mine = lax.dynamic_slice_in_dim(value_total, index_pb * row_count, row_count, 0)
    key_grad = (key_mine * factor).astype(jnp.bfloat16)
    value_grad = value_mine.astype(jnp.bfloat16)
    return (query_grad, key_grad, value_grad)


MESH = pl.DeviceIdType.MESH
NT = (((1,), (1,)), ((), ()))
TN = (((0,), (0,)), ((), ()))


def plane_kernel(
    rows, factor,
    q_in, k_in, v_in, o_in, g_in, lse_in, map_in,
    dq_out, dk_out, dv_out,
    q_buf, g_buf, k_buf, v_buf, o_buf, lse_buf, map_buf, stat,
    dq_acc, dk_acc, dv_acc,
    kv_send, kv_recv, dq_send, dq_recv,
    local_sem, send_sem, recv_sem,
):
    p = lax.axis_index("pb")
    x = lax.axis_index("ka")
    h = lax.axis_index("ha")
    c = lax.rem(p, 2)
    y = p // 2
    p_core = p + 1 - 2 * c
    p_far = lax.rem(p + 2, 4)
    to_core = (p_core, x, h)
    to_x = (p, 1 - x, h)
    to_y = (p_far, x, h)
    to_both = (p_core, 1 - x, h)
    fold_rows = rows // 2

    def part(slot):
        return pl.ds(slot * rows, rows)

    barrier = pltpu.get_barrier_semaphore()
    for peer in (to_core, to_x, to_y, to_both):
        pl.semaphore_signal(barrier, inc=1, device_id=peer, device_id_type=MESH)
    locals_ = []
    for n, (src, dst) in enumerate((
        (g_in, g_buf.at[part(0)]), (o_in, o_buf), (lse_in, lse_buf), (q_in, q_buf.at[part(0)]),
        (k_in, k_buf.at[part(0)]), (v_in, v_buf.at[part(0)]), (map_in, map_buf),
    )):
        copy = pltpu.make_async_copy(src, dst, local_sem.at[n])
        copy.start()
        locals_.append(copy)
    pl.semaphore_wait(barrier, 4)

    sends = []

    def send(n, src, dst, peer):
        copy = pltpu.make_async_remote_copy(
            src_ref=src, dst_ref=dst, send_sem=send_sem.at[n], recv_sem=recv_sem.at[n],
            device_id=peer, device_id_type=MESH,
        )
        copy.start()
        sends.append(copy)
        return copy

    q_x = send(0, q_in, q_buf.at[part(2)], to_x)
    k_y = send(1, k_in, k_buf.at[part(1)], to_y)
    q_c = send(2, q_in, q_buf.at[part(1)], to_core)
    g_c = send(3, g_in, g_buf.at[part(1)], to_core)
    g_x = send(4, g_in, g_buf.at[part(2)], to_x)
    v_y = send(5, v_in, v_buf.at[part(1)], to_y)

    for copy in locals_[:3]:
        copy.wait()
    gram = lax.dot_general(o_buf[...], g_buf[part(0)], NT, preferred_element_type=jnp.float32)
    down = lax.broadcasted_iota(jnp.int32, (rows, rows), 0)
    along = lax.broadcasted_iota(jnp.int32, (rows, rows), 1)
    delta = jnp.sum(jnp.where(down == along, gram, 0.0), axis=0, keepdims=True)
    delta = delta.astype(jnp.bfloat16).astype(jnp.float32)
    log2e = math.log2(math.e)
    lse = lse_buf[...].astype(jnp.float32) * log2e
    which = lax.broadcasted_iota(jnp.int32, (8, rows), 0)
    stat[0] = jnp.where(which == 0, lse, delta)
    st_c = send(6, stat.at[0], stat.at[1], to_core)
    st_x = send(7, stat.at[0], stat.at[2], to_x)
    st_b = send(8, stat.at[0], stat.at[3], to_both)
    for copy in locals_[3:]:
        copy.wait()

    q_owner = (p * 2 + x, p_core * 2 + x, p * 2 + 1 - x, p_core * 2 + 1 - x)
    k_owner = (p * 2 + x, p_far * 2 + x)
    half = lax.broadcasted_iota(jnp.int32, (1, rows), 1) // fold_rows
    lane = lax.broadcasted_iota(jnp.int32, (fold_rows, rows), 1) % fold_rows
    level = lax.broadcasted_iota(jnp.int32, (fold_rows, rows), 0)

    def span(slots):
        return pl.ds(slots[0] * rows, len(slots) * rows)

    def stat_row(n, slots):
        return jnp.concatenate([stat[s, n:n + 1, :] for s in slots], axis=1)

    def probabilities(keyed, asked, scores):
        own = keyed == [0] and asked == [0]
        q_fold = jnp.concatenate([
            jnp.where(half == 0, map_buf[q_owner[s] * 2], map_buf[q_owner[s] * 2 + 1])
            for s in asked], axis=1)
        lse_row = stat_row(0, asked)
        parts = []
        for n in range(2 * len(keyed)):
            k_fold = map_buf[k_owner[keyed[n // 2]] * 2 + n % 2]
            scaled = scores[n * fold_rows:(n + 1) * fold_rows] * (factor * log2e)
            if own:
                seen = k_fold * fold_rows + level <= q_fold * fold_rows + lane
                parts.append(jnp.where(seen, jnp.exp2(scaled - lse_row), 0.0))
            else:
                parts.append(jnp.exp2(scaled - jnp.where(q_fold > k_fold, lse_row, 1e30)))
        return parts

    def tile(keyed, asked, first_q, first_k, after_dv=None, after_dk=None):
        query, grad = q_buf[span(asked)], g_buf[span(asked)]
        scores = lax.dot_general(k_buf[span(keyed)], query, NT, preferred_element_type=jnp.float32)
        dprobs = lax.dot_general(v_buf[span(keyed)], grad, NT, preferred_element_type=jnp.float32)
        parts = probabilities(keyed, asked, scores)
        delta_row = stat_row(1, asked)
        lows = []
        for n in reversed(range(len(keyed))):
            j = keyed[n]
            probs = jnp.concatenate(parts[2 * n:2 * n + 2], axis=0)
            dv = jnp.dot(probs.astype(jnp.bfloat16), grad, preferred_element_type=jnp.float32)
            dv_acc[part(j)] = dv if first_k else dv_acc[part(j)] + dv
            if after_dv is not None and j == 1:
                after_dv()
            dscores = probs * (dprobs[n * rows:(n + 1) * rows] - delta_row)
            lows.insert(0, dscores.astype(jnp.bfloat16))
            dk = jnp.dot(lows[0], query, preferred_element_type=jnp.float32)
            dk_acc[part(j)] = dk if first_k else dk_acc[part(j)] + dk
            if after_dk is not None and j == 1:
                after_dk()
        low = jnp.concatenate(lows, axis=0)
        dq = lax.dot_general(low, k_buf[span(keyed)], TN, preferred_element_type=jnp.float32)
        dq_acc[span(asked)] = dq if first_q else dq_acc[span(asked)] + dq

    def send_dq(n, s, peer):
        dq_send[s - 1] = dq_acc[part(s)].astype(jnp.bfloat16)
        return send(n, dq_send.at[s - 1], dq_recv.at[s - 1], peer)

    def send_kv(n, i, acc):
        kv_send[i] = acc[part(1)].astype(jnp.bfloat16)
        return send(n, kv_send.at[i], kv_recv.at[i], to_y)

    tile([0], [0], True, True)
    q_x.wait_recv()
    q_r = send(9, q_buf.at[part(2)], q_buf.at[part(3)], to_core)
    g_x.wait_recv()
    g_r = send(10, g_buf.at[part(2)], g_buf.at[part(3)], to_core)
    q_c.wait_recv()
    g_c.wait_recv()
    st_c.wait_recv()
    tile([0], [1], True, False)
    k_y.wait_recv()
    v_y.wait_recv()
    tile([1], [0, 1], False, True)
    dq_1 = send_dq(11, 1, to_core)
    st_x.wait_recv()
    tile([1], [2], True, False)
    q_r.wait_recv()
    g_r.wait_recv()
    st_b.wait_recv()
    late = []
    tile([1], [3], True, False, lambda: late.append(send_kv(13, 0, dv_acc)),
         lambda: late.append(send_kv(14, 1, dk_acc)))
    tile([0], [2], False, False)
    dq_2 = send_dq(12, 2, to_x)
    tile([0], [3], False, False)
    dq_3 = send_dq(15, 3, to_both)
    dq_1.wait_recv()
    dq_2.wait_recv()
    dq_mine = (dq_acc[part(0)] + dq_recv[0].astype(jnp.float32)) + dq_recv[1].astype(jnp.float32)
    late[0].wait_recv()
    dv_out[...] = (dv_acc[part(0)] + kv_recv[0].astype(jnp.float32)).astype(jnp.bfloat16)
    late[1].wait_recv()
    dk_out[...] = (
        (dk_acc[part(0)] + kv_recv[1].astype(jnp.float32)) * factor).astype(jnp.bfloat16)
    dq_3.wait_recv()
    dq_out[...] = ((dq_mine + dq_recv[2].astype(jnp.float32)) * factor).astype(jnp.bfloat16)
    for copy in sends:
        copy.wait_send()


def store_kernel(dq_in, dk_in, dv_in, dq_out, dk_out, dv_out, sems):
    copies = []
    for n, (src, dst) in enumerate(((dq_in, dq_out), (dk_in, dk_out), (dv_in, dv_out))):
        copy = pltpu.make_async_copy(src, dst, sems.at[n])
        copy.start()
        copies.append(copy)
    for copy in copies:
        copy.wait()


def plane_body(queries, key_rows, value_rows, outputs, out_grad, saved_lse, fold_map):
    rows, width = queries.shape
    factor = 1.0 / math.sqrt(width)
    low, full = jnp.bfloat16, jnp.float32
    grad = jax.ShapeDtypeStruct((rows, width), low)
    arrays = [
        pltpu.with_memory_space_constraint(a, pltpu.HBM)
        for a in (queries, key_rows, value_rows, outputs, out_grad, saved_lse.reshape(1, rows),
                  fold_map)
    ]
    grads = pl.pallas_call(
        functools.partial(plane_kernel, rows, factor),
        out_shape=(pltpu.VMEM((rows, width), low),) * 3,
        in_specs=[pl.BlockSpec(memory_space=pl.ANY)] * 7,
        out_specs=[pl.BlockSpec(memory_space=pltpu.VMEM)] * 3,
        scratch_shapes=[
            pltpu.VMEM((4 * rows, width), low),
            pltpu.VMEM((4 * rows, width), low),
            pltpu.VMEM((2 * rows, width), low),
            pltpu.VMEM((2 * rows, width), low),
            pltpu.VMEM((rows, width), low),
            pltpu.VMEM((1, rows), low),
            pltpu.SMEM(fold_map.shape, jnp.int32),
            pltpu.VMEM((4, 8, rows), full),
            pltpu.VMEM((4 * rows, width), full),
            pltpu.VMEM((2 * rows, width), full),
            pltpu.VMEM((2 * rows, width), full),
            pltpu.VMEM((2, rows, width), low),
            pltpu.VMEM((2, rows, width), low),
            pltpu.VMEM((3, rows, width), low),
            pltpu.VMEM((3, rows, width), low),
            pltpu.SemaphoreType.DMA((7,)),
            pltpu.SemaphoreType.DMA((16,)),
            pltpu.SemaphoreType.DMA((16,)),
        ],
        compiler_params=pltpu.CompilerParams(
            collective_id=0, has_side_effects=True, vmem_limit_bytes=32 * 2**20
        ),
        cost_estimate=pl.CostEstimate(
            flops=80 * rows * rows * width,
            bytes_accessed=16 * rows * width,
            transcendentals=8 * rows * rows,
        ),
    )(*arrays)
    return pl.pallas_call(
        store_kernel,
        out_shape=(grad, grad, grad),
        in_specs=[pl.BlockSpec(memory_space=pl.ANY)] * 3,
        out_specs=[pl.BlockSpec(memory_space=pl.ANY)] * 3,
        scratch_shapes=[pltpu.SemaphoreType.DMA((3,))],
        compiler_params=pltpu.CompilerParams(vmem_limit_bytes=2**20),
    )(*[pltpu.with_memory_space_constraint(a, pltpu.VMEM) for a in grads])


def solution(mesh):
    plane = mesh.shape["pb"] == 4 and mesh.shape["ka"] == 2
    return jax.shard_map(
        plane_body if plane else body,
        mesh=mesh,
        in_specs=(
            P(("pb", "ka"), "ha"),
            P(("pb", "ka"), "ha"),
            P(("pb", "ka"), "ha"),
            P(("pb", "ka"), "ha"),
            P(("pb", "ka"), "ha"),
            P(("pb", "ka"), "ha"),
            P(),
        ),
        out_specs=(P(("pb", "ka"), "ha"), P(("pb", "ka"), "ha"), P(("pb", "ka"), "ha")),
        check_vma=False,
    )
```
